32 devices in a mesh: dp: 8 (over z, x), mp: 4 (over y, core).
Axes of the slice: x: 2, y: 2, z: 4, core: 2. Of those that a mesh axis runs over, the one named last changes fastest.
Arguments:
- tokens: bfloat16 [12288, 768], P('dp'), may hold values from -6 to 6
- lengths: int32 [8, 2], P('dp'), may hold values from 0 to 1536, as said below
- w_query: bfloat16 [768, 768], P(None, 'mp'), may hold values from -0.21875 to 0.21875
- b_query: float32 [768], P('mp'), may hold values from -3 to 3
- w_key: bfloat16 [768, 768], P(None, 'mp'), may hold values from -0.21875 to 0.21875
- b_key: float32 [768], P('mp'), may hold values from -3 to 3
- w_value: bfloat16 [768, 768], P(None, 'mp'), may hold values from -0.21875 to 0.21875
- b_value: float32 [768], P('mp'), may hold values from -3 to 3
- w_out: bfloat16 [768, 768], P('mp'), may hold values from -1.75 to 1.75
- b_out: float32 [768], replicated, may hold values from -3 to 3
- ln1_gain: float32 [768], replicated, may hold values from 0.5 to 1.5
- ln1_bias: float32 [768], replicated, may hold values from -3 to 3
- w_in: bfloat16 [768, 3072], P('dp', 'mp'), may hold values from -0.21875 to 0.21875
- b_in: float32 [3072], P('mp'), may hold values from -3 to 3
- w_down: bfloat16 [3072, 768], P('mp', 'dp'), may hold values from -0.109375 to 0.109375
- b_down: float32 [768], replicated, may hold values from -3 to 3
- ln2_gain: float32 [768], replicated, may hold values from 0.5 to 1.5
- ln2_bias: float32 [768], replicated, may hold values from -3 to 3
- cotangent: float32 [12288, 768], P('dp'), may hold values from -6 to 6
Outputs:
- layer_out: bfloat16 [12288, 768], P('dp')
- grad_tokens: float32 [12288, 768], P('dp', 'mp')
- grad_w_query: float32 [768, 768], P(None, 'mp')
- grad_b_query: float32 [768], P('mp')
- grad_w_key: float32 [768, 768], P(None, 'mp')
- grad_b_key: float32 [768], P('mp')
- grad_w_value: float32 [768, 768], P(None, 'mp')
- grad_b_value: float32 [768], P('mp')
- grad_w_out: float32 [768, 768], P('mp')
- grad_b_out: float32 [768], replicated
- grad_ln1_gain: float32 [768], replicated
- grad_ln1_bias: float32 [768], replicated
- grad_w_in: float32 [768, 3072], P('dp', 'mp')
- grad_b_in: float32 [3072], P('mp')
- grad_w_down: float32 [3072, 768], P('mp', 'dp')
- grad_b_down: float32 [768], replicated
- grad_ln2_gain: float32 [768], replicated
- grad_ln2_bias: float32 [768], replicated
The draws below stay inside these ranges and needn't reach their ends.
Inputs may be any that keep to these rules, and one draw needn't show every extreme that they name: Row r holds a sequence of lengths[r, 0] tokens from slot 0, at least 64, then a second sequence of lengths[r, 1] tokens (0, or at least 64), then padding; lengths[r, 0] + lengths[r, 1] <= 1536; some row holds one sequence of all 1536 slots.
All inputs are finite; a program needn't handle non-finite values.
Results may differ from the reference program's by a relative error of at most 0.03.
Values may be sent and summed in bfloat16 or wider, within the bound.
No kernel may reach another device: no remote copies, remote signals or barrier semaphores. Data moves between devices by JAX's collectives and lax.ppermute only.
A program may use at most 192 MiB of HBM per device.

```python
import math
import jax
import jax.numpy as jnp
from jax import lax

D = 768
HEADS = 12
HEAD_DIM = 64
FF = 3072
SLOTS = 1536
MINLEN = 64
ROWS = 8
TOKENS = 12288
N_MP = 4


def draw_lengths(key, part):
    key = jax.random.fold_in(key, 7)
    keys = jax.random.split(key, 5)
    shape = (ROWS,)
    first_len = jnp.minimum(jnp.minimum(jax.random.randint(keys[0], shape, MINLEN, SLOTS + 1), jax.random.randint(keys[1], shape, MINLEN, SLOTS + 1)), jax.random.randint(keys[2], shape, MINLEN, SLOTS + 1))
    room = SLOTS - first_len
    second_len = MINLEN + jax.random.randint(keys[3], shape, 0, jnp.maximum(room - MINLEN + 1, 1))
    second_len = jnp.where(room >= MINLEN, second_len, 0)
    chosen = jax.random.randint(keys[4], (), 0, ROWS)
    picked = jnp.arange(ROWS) == chosen
    first_len = jnp.where(picked, SLOTS, first_len)
    second_len = jnp.where(picked, 0, second_len)
    return jnp.stack([first_len, second_len], axis=1).astype(jnp.int32)


def shard_levels(rng, extent, cuts, least, top_value):
    factor_of = 1.0
    for position, shards_of in cuts:
        heights = jax.random.uniform(jax.random.fold_in(jax.random.fold_in(rng, 6), position), (shards_of,), jnp.float32, least / len(cuts), top_value / len(cuts))
        factor_of = factor_of * jnp.repeat(jnp.exp(heights), extent[position] // shards_of).reshape((-1,) + (1,) * (len(extent) - 1 - position))
    return factor_of


def bell_draw(key, extent, scale, limit, shards=(), kind=jnp.bfloat16):
    gain = shard_levels(key, extent, shards, -0.22, 0.18) if shards else 1.0
    values = jax.random.normal(key, extent, jnp.float32) * scale * gain
    return jnp.minimum(jnp.maximum(values, -limit), limit).astype(kind)


def setup_inputs(seed: int = 0) -> dict:
    key_list = jax.random.split(jax.random.key(seed), 20)
    return {
        "tokens": bell_draw(key_list[0], (TOKENS, D), 1.0, 6.0, ((0, 8),)),
        "lengths": draw_lengths(jax.random.fold_in(key_list[19], 71), 0),
        "w_query": bell_draw(key_list[2], (D, D), D ** -0.5, 0.21875, ((1, 4),)),
        "b_query": bell_draw(key_list[3], (D,), 0.5, 3.0, ((0, 4),), jnp.float32),
        "w_key": bell_draw(key_list[4], (D, D), D ** -0.5, 0.21875, ((1, 4),)),
        "b_key": bell_draw(key_list[5], (D,), 0.5, 3.0, ((0, 4),), jnp.float32),
        "w_value": bell_draw(key_list[6], (D, D), D ** -0.5, 0.21875, ((1, 4),)),
        "b_value": bell_draw(key_list[7], (D,), 0.5, 3.0, ((0, 4),), jnp.float32),
        "w_out": bell_draw(key_list[8], (D, D), (D // 64) ** -0.5, 1.75, ((0, 4),)),
        "b_out": bell_draw(key_list[9], (D,), 0.5, 3.0, (), jnp.float32),
        "ln1_gain": jnp.clip(1.0 + 0.1 * jax.random.normal(key_list[10], (D,), jnp.float32), 0.5, 1.5),
        "ln1_bias": bell_draw(key_list[11], (D,), 0.5, 3.0, (), jnp.float32),
        "w_in": bell_draw(key_list[12], (D, FF), D ** -0.5, 0.21875, ((0, 8), (1, 4))),
        "b_in": bell_draw(key_list[13], (FF,), 0.5, 3.0, ((0, 4),), jnp.float32),
        "w_down": bell_draw(key_list[14], (FF, D), FF ** -0.5, 0.109375, ((0, 4), (1, 8))),
        "b_down": bell_draw(key_list[15], (D,), 0.5, 3.0, (), jnp.float32),
        "ln2_gain": jnp.clip(1.0 + 0.1 * jax.random.normal(key_list[16], (D,), jnp.float32), 0.5, 1.5),
        "ln2_bias": bell_draw(key_list[17], (D,), 0.5, 3.0, (), jnp.float32),
        "cotangent": bell_draw(key_list[18], (TOKENS, D), 1.0, 6.0, ((0, 8),), jnp.float32),
    }


@jax.custom_vjp
def low(v):
    return lax.optimization_barrier(v.astype(jnp.bfloat16)).astype(jnp.float32)

@jax.custom_vjp
def low_back(v):
    return v

def low_keep(v):
    return (low(v), None)

def low_pass(kept, grad):
    return (grad,)

def back_keep(v):
    return (v, None)

def back_low(kept, grad):
    return (low(grad),)
low.defvjp(low_keep, low_pass)
low_back.defvjp(back_keep, back_low)
norm_eps = 1e-12
masked_score = -1e+30
highest = lax.Precision.HIGHEST

def layer_norm(summed, gain_vec, shift_vec):
    center = summed - lax.optimization_barrier(jnp.mean(summed, axis=-1, keepdims=True))
    spread = lax.optimization_barrier(jnp.mean(center * center, axis=-1, keepdims=True))
    return center * lax.rsqrt(spread + norm_eps) * gain_vec + shift_vec

def rotary_tables(lengths):
    places = jnp.arange(SLOTS, dtype=jnp.int32)[None, :]
    first_len = lengths[:, 0:1]
    used_len = first_len + lengths[:, 1:2]
    segment = (places >= first_len).astype(jnp.int32) + (places >= used_len).astype(jnp.int32)
    starts = jnp.where(segment == 0, 0, jnp.where(segment == 1, first_len, used_len))
    offsets = (places - starts).astype(jnp.float32)
    halfdim = HEAD_DIM // 2
    frequency = jnp.exp(jnp.arange(halfdim, dtype=jnp.float32) * (-math.log(10000.0) / halfdim))
    frequency = jnp.concatenate([frequency, frequency])
    angles = offsets[:, :, None, None] * frequency
    return (segment, jnp.cos(angles), jnp.sin(angles))

def rotate(vectors, cosine_tab, sine_tab):
    halfdim = vectors.shape[-1] // 2
    turned = jnp.concatenate([-vectors[..., halfdim:], vectors[..., :halfdim]], axis=-1)
    return vectors * cosine_tab + turned * sine_tab

def row_layer(row_in, row_seg, row_cos, row_sin, params):
    w_query, b_query, w_key, b_key, w_value, b_value, w_out, b_out, ln1_gain, ln1_bias, w_in, b_in, w_down, b_down, ln2_gain, ln2_bias = params

    def project(weight, shift_vec):
        linear = low_back(jnp.dot(row_in, weight, precision=highest) + shift_vec)
        return linear.reshape(SLOTS, HEADS, HEAD_DIM)
    queries = low(rotate(project(w_query, b_query), row_cos, row_sin))
    keyset = low(rotate(project(w_key, b_key), row_cos, row_sin))
    values = low(project(w_value, b_value))
    score_scale = 1.0 / math.sqrt(HEAD_DIM)
    scores = jnp.einsum('qhd,khd->hqk', queries, keyset, precision=highest) * score_scale
    allowed = (row_seg[:, None] == row_seg[None, :])[None]
    scores = low_back(jnp.where(allowed, scores, masked_score))
    weights = low(jax.nn.softmax(scores, axis=-1))
    attn_mix = jnp.einsum('hqk,khd->qhd', weights, values, precision=highest)
    attn_mix = low(low_back(attn_mix)).reshape(SLOTS, D)
    group_width = D // N_MP
    attended = jnp.zeros((SLOTS, D), jnp.float32)
    for group_idx in range(N_MP):
        start_col = group_idx * group_width
        partial_out = jnp.dot(attn_mix[:, start_col:start_col + group_width], w_out[start_col:start_col + group_width], precision=highest)
        attended = attended + low(partial_out)
    attended = low_back(attended)
    normed_one = layer_norm(row_in + attended + b_out, ln1_gain, ln1_bias)
    normed_low = low(normed_one)
    hidden_width = FF // N_MP
    result = jnp.zeros((SLOTS, D), jnp.float32)
    for group_idx in range(N_MP):
        start_col = group_idx * hidden_width
        inner_pre = low_back(jnp.dot(normed_low, w_in[:, start_col:start_col + hidden_width], precision=highest) + b_in[start_col:start_col + hidden_width])
        active = low(jax.nn.gelu(inner_pre, approximate=False))
        result = result + low(jnp.dot(active, w_down[start_col:start_col + hidden_width], precision=highest))
    result = low_back(result)
    return layer_norm(normed_one + result + b_down, ln2_gain, ln2_bias)

def reference(tokens, lengths, w_query, b_query, w_key, b_key, w_value, b_value, w_out, b_out, ln1_gain, ln1_bias, w_in, b_in, w_down, b_down, ln2_gain, ln2_bias, cotangent):
    segment, cosine_tab, sine_tab = rotary_tables(lengths)
    params = tuple((item.astype(jnp.float32) for item in (w_query, b_query, w_key, b_key, w_value, b_value, w_out, b_out, ln1_gain, ln1_bias, w_in, b_in, w_down, b_down, ln2_gain, ln2_bias)))
    inputs = tokens.astype(jnp.float32).reshape(ROWS, SLOTS, D)

    def forward(inputs, params):

        def one_row(row_items):
            row_in, row_seg, row_cos, row_sin = row_items
            return row_layer(row_in, row_seg, row_cos, row_sin, params)
        return lax.map(jax.checkpoint(one_row), (inputs, segment, cosine_tab, sine_tab))
    outputs, pullback = jax.vjp(forward, inputs, params)
    valid_rows = (segment < 2)[:, :, None]
    seed_grad = jnp.where(valid_rows, cotangent.astype(jnp.float32).reshape(ROWS, SLOTS, D), 0.0)
    grad_inputs, grads = pullback(seed_grad)
    return (outputs.reshape(TOKENS, D).astype(jnp.bfloat16), grad_inputs.reshape(TOKENS, D), grads[0], grads[1], grads[2], grads[3], grads[4], grads[5], grads[6], grads[7], grads[8], grads[9], grads[10], grads[11], grads[12], grads[13], grads[14], grads[15])
```

```python
import math

import jax
import jax.numpy as jnp
from jax import lax
from jax.experimental import pallas as pl
from jax.experimental.pallas import tpu as pltpu
from jax.sharding import PartitionSpec as P

HEAD_DIM = 64
HALF_DIM = HEAD_DIM // 2
WIDE = 128
USED = 80
MASKED = -1e30
LOG2E = math.log2(math.e)
EPS = 1e-12
BLOCK = 256
bf16 = jnp.bfloat16
f32 = jnp.float32
VMEM = pl.BlockSpec(memory_space=pltpu.VMEM)
SMEM = pl.BlockSpec(memory_space=pltpu.SMEM)


def params(mib=56):
    return pltpu.CompilerParams(vmem_limit_bytes=mib * 2**20)


def out(*shape, dtype=bf16):
    return jax.ShapeDtypeStruct(shape, dtype)


def fixed(*shape):
    return pl.BlockSpec(shape, lambda i, *_: (0,) * len(shape))


def dot(left, right, left_dim, right_dim):
    return lax.dot_general(
        left, right, (((left_dim,), (right_dim,)), ((), ())), preferred_element_type=f32
    )


def qkv_body(
    len_ref, tok_ref, wq_ref, wk_ref, wv_ref, bq_ref, bk_ref, bv_ref, freq_ref,
    qa_ref, ka_ref, va_ref, cos_ref, sin_ref,
):
    n = tok_ref.shape[0]
    heads = wq_ref.shape[0] // HEAD_DIM
    pos = lax.broadcasted_iota(jnp.int32, (1, n), 1)
    first = len_ref[0, 0]
    used = first + len_ref[0, 1]
    in0, in1 = pos < first, pos < used
    start = jnp.where(in0, 0, jnp.where(in1, first, used))
    angles = freq_ref[...] * (pos - start).astype(f32)
    cosine, sine = jnp.cos(angles), jnp.sin(angles)
    cos_ref[...] = cosine
    sin_ref[...] = sine
    segment = jnp.where(in0, 0, jnp.where(in1, 1, 2))
    row = lax.broadcasted_iota(jnp.int32, (WIDE - HEAD_DIM, n), 0)
    same = row == segment
    q_tail = jnp.where(same, 1.0, 0.0).astype(bf16)
    k_tail = jnp.where(jnp.logical_or(same, row > 2), 0.0, MASKED).astype(bf16)
    v_tail = jnp.where(row < 3, 1.0, 0.0).astype(bf16)
    tok = tok_ref[...]

    def rotated(lin, h, scale):
        a = lin[h * HEAD_DIM : h * HEAD_DIM + HALF_DIM]
        b = lin[h * HEAD_DIM + HALF_DIM : (h + 1) * HEAD_DIM]
        x, y = a * cosine - b * sine, b * cosine + a * sine
        if scale != 1.0:
            x, y = x * scale, y * scale
        return x.astype(bf16), y.astype(bf16)

    for w_ref, b_ref, to_ref, tail, scale in (
        (wq_ref, bq_ref, qa_ref, q_tail, LOG2E / math.sqrt(HEAD_DIM)),
        (wk_ref, bk_ref, ka_ref, k_tail, 1.0),
        (wv_ref, bv_ref, va_ref, v_tail, None),
    ):
        lin = dot(w_ref[...], tok, 1, 1) + b_ref[...]
        for h in range(heads):
            if scale is None:
                to_ref[h, 0:HEAD_DIM] = lin[h * HEAD_DIM : (h + 1) * HEAD_DIM].astype(bf16)
            else:
                x, y = rotated(lin, h, scale)
                to_ref[h, 0:HALF_DIM] = x
                to_ref[h, HALF_DIM:HEAD_DIM] = y
            to_ref[h, HEAD_DIM:] = tail


def project(lengths, tok, wq, wk, wv, bq, bk, bv):
    n = tok.shape[0]
    heads = wq.shape[0] // HEAD_DIM
    freq = jnp.exp(jnp.arange(HALF_DIM, dtype=f32) * (-math.log(10000.0) / HALF_DIM))
    return pl.pallas_call(
        qkv_body,
        out_shape=(
            out(heads, WIDE, n), out(heads, WIDE, n), out(heads, WIDE, n),
            out(HALF_DIM, n, dtype=f32), out(HALF_DIM, n, dtype=f32),
        ),
        in_specs=[SMEM] + [VMEM] * 8,
        out_specs=(VMEM,) * 5,
        compiler_params=params(),
    )(
        lengths, tok, wq, wk, wv,
        bq.reshape(-1, 1), bk.reshape(-1, 1), bv.reshape(-1, 1), freq.reshape(-1, 1),
    )


def attend_body(qa_ref, ka_ref, va_ref, p_ref, mix_ref, inv_ref):
    for h in range(qa_ref.shape[0]):
        scores = dot(ka_ref[h], qa_ref[h], 0, 0)
        top = jnp.max(scores, axis=0, keepdims=True)
        p = jnp.exp2(scores - top).astype(bf16)
        p_ref[h] = p
        mixed = jnp.dot(va_ref[h, 0:USED], p, preferred_element_type=f32)
        inv = 1.0 / mixed[HEAD_DIM : HEAD_DIM + 1]
        mix_ref[h * HEAD_DIM : (h + 1) * HEAD_DIM] = (mixed[0:HEAD_DIM] * inv).astype(bf16)
        inv_ref[h] = inv


def attend(qa, ka, va):
    heads, _, n = qa.shape
    return pl.pallas_call(
        attend_body,
        grid=(n // BLOCK,),
        in_specs=[
            pl.BlockSpec((heads, WIDE, BLOCK), lambda i: (0, 0, i)),
            fixed(heads, WIDE, n),
            fixed(heads, WIDE, n),
        ],
        out_specs=(
            pl.BlockSpec((heads, n, BLOCK), lambda i: (0, 0, i)),
            pl.BlockSpec((heads * HEAD_DIM, BLOCK), lambda i: (0, i)),
            pl.BlockSpec((heads, 1, BLOCK), lambda i: (0, 0, i)),
        ),
        out_shape=(out(heads, n, n), out(heads * HEAD_DIM, n), out(heads, 1, n, dtype=f32)),
        compiler_params=params(),
    )(qa, ka, va)


def attend_back_body(
    do_ref, mix_ref, inv_ref, qa_ref, ka_ref, va_ref, p_ref, cos_ref, sin_ref, cos_all, sin_all,
    dq_ref, dkv_ref, dk_acc, dv_acc,
):
    heads, _, width = qa_ref.shape
    step = pl.program_id(0)

    @pl.when(step == 0)
    def _():
        dk_acc[...] = jnp.zeros_like(dk_acc)
        dv_acc[...] = jnp.zeros_like(dv_acc)

    def turned_back(a, b, cosine, sine):
        return (a * cosine + b * sine).astype(bf16), (b * cosine - a * sine).astype(bf16)

    for h in range(heads):
        lo, mid, hi = h * HEAD_DIM, h * HEAD_DIM + HALF_DIM, (h + 1) * HEAD_DIM
        do = (do_ref[lo:hi].astype(f32) * inv_ref[h]).astype(bf16)
        delta = jnp.sum(do.astype(f32) * mix_ref[lo:hi].astype(f32), axis=0, keepdims=True)
        d1 = delta.astype(bf16).astype(f32)
        d2 = (delta - d1).astype(bf16).astype(f32)
        d3 = delta - d1 - d2
        row = lax.broadcasted_iota(jnp.int32, (USED - HEAD_DIM, width), 0)
        tail = jnp.where(row == 0, -d1, jnp.where(row == 1, -d2, jnp.where(row == 2, -d3, 0.0)))
        do_wide = jnp.concatenate([do, tail.astype(bf16)], axis=0)
        dp = dot(va_ref[h, 0:USED], do_wide, 0, 0)
        p = p_ref[h]
        ds = p * dp.astype(bf16)
        dq = jnp.dot(ka_ref[h, 0:HEAD_DIM], ds, preferred_element_type=f32)
        dq = dq * (1.0 / math.sqrt(HEAD_DIM))
        x, y = turned_back(dq[0:HALF_DIM], dq[HALF_DIM:HEAD_DIM], cos_ref[...], sin_ref[...])
        dq_ref[lo:mid] = x
        dq_ref[mid:hi] = y
        dk_acc[lo:hi] += dot(qa_ref[h, 0:HEAD_DIM], ds, 1, 1)
        dv_acc[lo:hi] += dot(do, p, 1, 1)

    @pl.when(step == pl.num_programs(0) - 1)
    def _():
        w = heads * HEAD_DIM
        for h in range(heads):
            lo, mid, hi = h * HEAD_DIM, h * HEAD_DIM + HALF_DIM, (h + 1) * HEAD_DIM
            a, b = dk_acc[lo:mid] * math.log(2.0), dk_acc[mid:hi] * math.log(2.0)
            x, y = turned_back(a, b, cos_all[...], sin_all[...])
            dkv_ref[lo:mid] = x
            dkv_ref[mid:hi] = y
        dkv_ref[w:] = dv_acc[...].astype(bf16)


def attend_back(do, mix, inv, qa, ka, va, p, cosine, sine):
    heads, _, n = qa.shape
    w = heads * HEAD_DIM
    columns = pl.BlockSpec((w, BLOCK), lambda i: (0, i))
    table = pl.BlockSpec((HALF_DIM, BLOCK), lambda i: (0, i))
    return pl.pallas_call(
        attend_back_body,
        grid=(n // BLOCK,),
        in_specs=[
            columns,
            columns,
            pl.BlockSpec((heads, 1, BLOCK), lambda i: (0, 0, i)),
            pl.BlockSpec((heads, WIDE, BLOCK), lambda i: (0, 0, i)),
            fixed(heads, WIDE, n),
            fixed(heads, WIDE, n),
            pl.BlockSpec((heads, n, BLOCK), lambda i: (0, 0, i)),
            table,
            table,
            fixed(HALF_DIM, n),
            fixed(HALF_DIM, n),
        ],
        out_specs=(columns, fixed(2 * w, n)),
        out_shape=(out(w, n), out(2 * w, n)),
        scratch_shapes=[pltpu.VMEM((w, n), f32), pltpu.VMEM((w, n), f32)],
        compiler_params=params(),
    )(do, mix, inv, qa, ka, va, p, cosine, sine, cosine, sine)


def near(shape, blocks):
    return pl.BlockSpec(shape, lambda i, *_: (jnp.minimum(i, blocks - 1), 0))


def far(shape, blocks):
    return pl.BlockSpec(shape, lambda i, *_: (jnp.maximum(i - blocks, 0), 0))


def true_block(i, where, blocks):
    return lax.rem(i + where[0] * blocks, 2 * blocks)


def forward_body(
    where_ref, order_ref, mix_a, mix_b, wo_a, wo_b, tok_ref, bo_ref, gain_ref, shift_ref,
    near_ref, far_ref, bi_ref,
    low_ref, unit_ref, scale_ref, act_ref, slope_ref, own_ref, other_ref, wi_ref, wd_ref,
):
    step = pl.program_id(0)
    half = pl.num_programs(0) // 2

    @pl.when(step == 0)
    def _():
        parts = order_ref.shape[0]
        rows = wi_ref.shape[0] // parts
        for j in range(parts):
            from_ref, k = (near_ref, j) if j < near_ref.shape[0] else (far_ref, j - near_ref.shape[0])
            at = pl.ds(pl.multiple_of(order_ref[j] * rows, rows), rows)
            wi_ref[at] = from_ref[k, 0]
            wd_ref[at] = from_ref[k, 1]

    z = tok_ref[...].astype(f32) + dot(mix_a[...], wo_a[...], 0, 0) + dot(mix_b[...], wo_b[...], 0, 0)
    z = z + bo_ref[...]
    center = z - jnp.mean(z, axis=-1, keepdims=True)
    scale = lax.rsqrt(jnp.mean(center * center, axis=-1, keepdims=True) + EPS)
    unit = center * scale
    low = (unit * gain_ref[...] + shift_ref[...]).astype(bf16)
    low_ref[...] = low
    unit_ref[...] = unit
    scale_ref[...] = scale
    inner = jnp.dot(low, wi_ref[...], preferred_element_type=f32) + bi_ref[...]
    phi = 0.5 * lax.erf(inner * math.sqrt(0.5)) + 0.5
    act = (inner * phi).astype(bf16)
    bell = jnp.exp2(inner * inner * (-0.5 * LOG2E)) * (1.0 / math.sqrt(2.0 * math.pi))
    act_ref[...] = act
    slope_ref[...] = (phi + inner * bell).astype(bf16)
    part = dot(act, wd_ref[...], 1, 1).astype(bf16)

    @pl.when(step < half)
    def _():
        own_ref[...] = part

    @pl.when(step >= half)
    def _():
        other_ref[...] = part


def feed_forward(where, order, mix_a, mix_b, wo_a, wo_b, tok, bo, gain, shift, w_near, w_far, bi):
    n, d = tok.shape
    hidden = bi.shape[1]
    blocks = n // BLOCK // 2
    w2 = mix_a.shape[0]
    columns = pl.BlockSpec((w2, BLOCK), lambda i, where, order: (0, true_block(i, where, blocks)))
    rows = pl.BlockSpec((BLOCK, d), lambda i, where, order: (i, 0))
    wide = pl.BlockSpec((BLOCK, hidden), lambda i, where, order: (i, 0))
    return pl.pallas_call(
        forward_body,
        grid_spec=pltpu.PrefetchScalarGridSpec(
            num_scalar_prefetch=2,
            grid=(2 * blocks,),
            in_specs=[
                columns, columns, fixed(w2, d), fixed(w2, d),
                pl.BlockSpec((BLOCK, d), lambda i, where, order: (true_block(i, where, blocks), 0)),
                fixed(1, d), fixed(1, d), fixed(1, d),
                fixed(*w_near.shape), fixed(*w_far.shape), fixed(1, hidden),
            ],
            out_specs=(
                rows, rows, pl.BlockSpec((BLOCK, 1), lambda i, where, order: (i, 0)), wide, wide,
                near((BLOCK, d), blocks), far((BLOCK, d), blocks),
                fixed(d, hidden), fixed(d, hidden),
            ),
        ),
        out_shape=(
            out(n, d), out(n, d, dtype=f32), out(n, 1, dtype=f32), out(n, hidden), out(n, hidden),
            out(n // 2, d), out(n // 2, d), out(d, hidden), out(d, hidden),
        ),
        compiler_params=params(),
    )(where, order, mix_a, mix_b, wo_a, wo_b, tok, bo, gain, shift, w_near, w_far, bi)


def norm_back(g, unit, scale, gain):
    q = g * gain
    return scale * (
        q - jnp.mean(q, axis=-1, keepdims=True) - unit * jnp.mean(q * unit, axis=-1, keepdims=True)
    )


def column_sums(sums_ref, *terms):
    @pl.when(pl.program_id(0) == 0)
    def _():
        sums_ref[...] = jnp.zeros_like(sums_ref)

    for k, term in enumerate(terms):
        sums_ref[k : k + 1] += jnp.sum(term, axis=0, keepdims=True)


def second_norm_body(
    where_ref, len_ref, unit_ref, gain1_ref, shift1_ref, mine_ref, theirs_ref, bd_ref, gain_ref,
    shift_ref, cot_ref, out_ref, low_ref, sums_ref,
):
    step = pl.program_id(0)
    rows = unit_ref.shape[0]
    total = mine_ref[...].astype(f32) + theirs_ref[...].astype(f32)
    z = unit_ref[...] * gain1_ref[...] + shift1_ref[...] + total + bd_ref[...]
    center = z - jnp.mean(z, axis=-1, keepdims=True)
    scale = lax.rsqrt(jnp.mean(center * center, axis=-1, keepdims=True) + EPS)
    unit = center * scale
    out_ref[...] = (unit * gain_ref[...] + shift_ref[...]).astype(bf16)
    place = (where_ref[0] * pl.num_programs(0) + step) * rows
    place = place + lax.broadcasted_iota(jnp.int32, (rows, 1), 0)
    g = jnp.where(place < len_ref[0, 0] + len_ref[0, 1], cot_ref[...], 0.0)
    back = norm_back(g, unit, scale, gain_ref[...])
    low_ref[...] = back.astype(bf16)
    column_sums(sums_ref, g * unit, g, back)


def second_norm(where, lengths, unit, gain1, shift1, mine, theirs, bd, gain, shift, cot):
    n, d = cot.shape
    blocks = n // BLOCK // 2
    rows = pl.BlockSpec((BLOCK, d), lambda i, where, lens: (i, 0))
    return pl.pallas_call(
        second_norm_body,
        grid_spec=pltpu.PrefetchScalarGridSpec(
            num_scalar_prefetch=2,
            grid=(blocks,),
            in_specs=[
                rows, fixed(1, d), fixed(1, d), rows, rows, fixed(1, d), fixed(1, d), fixed(1, d),
                pl.BlockSpec((BLOCK, d), lambda i, where, lens: (where[0] * blocks + i, 0)),
            ],
            out_specs=(rows, rows, fixed(8, d)),
        ),
        out_shape=(out(n // 2, d), out(n // 2, d), out(8, d, dtype=f32)),
        compiler_params=params(),
    )(where, lengths, unit, gain1, shift1, mine, theirs, bd, gain, shift, cot)


def first_norm_body(unit_ref, scale_ref, gain_ref, skip_ref, mine_ref, theirs_ref, low_ref, sums_ref):
    g = skip_ref[...].astype(f32) + (mine_ref[...].astype(f32) + theirs_ref[...].astype(f32))
    unit = unit_ref[...]
    back = norm_back(g, unit, scale_ref[...], gain_ref[...])
    low_ref[...] = back.astype(bf16)
    column_sums(sums_ref, g * unit, g, back)


def first_norm(unit, scale, gain, skip, mine, theirs):
    half, d = skip.shape
    rows = pl.BlockSpec((BLOCK, d), lambda i: (i, 0))
    return pl.pallas_call(
        first_norm_body,
        grid=(half // BLOCK,),
        in_specs=[rows, pl.BlockSpec((BLOCK, 1), lambda i: (i, 0)), fixed(1, d), rows, rows, rows],
        out_specs=(rows, fixed(8, d)),
        out_shape=(out(half, d), out(8, d, dtype=f32)),
        compiler_params=params(),
    )(unit, scale, gain, skip, mine, theirs)


def backward_body(near_ref, far_ref, wi_ref, wd_ref, slope_ref, gi_ref, own_ref, other_ref, sums_ref):
    step = pl.program_id(0)
    half = pl.num_programs(0) // 2

    def run(from_ref, to_ref):
        g = jnp.dot(from_ref[...], wd_ref[...], preferred_element_type=f32)
        g = (g * slope_ref[...].astype(f32)).astype(bf16)
        gi_ref[...] = g
        to_ref[...] = dot(g, wi_ref[...], 1, 1).astype(bf16)
        column_sums(sums_ref, g.astype(f32))

    @pl.when(step < half)
    def _():
        run(near_ref, own_ref)

    @pl.when(step >= half)
    def _():
        run(far_ref, other_ref)


def feed_back(low_near, low_far, wi, wd, slope):
    n, hidden = slope.shape
    half, d = low_near.shape
    blocks = half // BLOCK
    wide = pl.BlockSpec((BLOCK, hidden), lambda i: (i, 0))
    return pl.pallas_call(
        backward_body,
        grid=(2 * blocks,),
        in_specs=[
            near((BLOCK, d), blocks), far((BLOCK, d), blocks), fixed(d, hidden), fixed(d, hidden), wide,
        ],
        out_specs=(wide, near((BLOCK, d), blocks), far((BLOCK, d), blocks), fixed(8, hidden)),
        out_shape=(out(n, hidden), out(half, d), out(half, d), out(8, hidden, dtype=f32)),
        compiler_params=params(),
    )(low_near, low_far, wi, wd, slope)


def weight_grad_body(order_ref, low_ref, gi_ref, near_ref, far_ref, act_ref, *refs):
    *to_refs, grad_ref = refs
    half = near_ref.shape[0]

    def spread(which):
        first = to_refs[0].shape[0]
        rows = to_refs[0].shape[2]
        for j in range(order_ref.shape[0]):
            to_ref, k = (to_refs[0], j) if j < first else (to_refs[1], j - first)
            at = pl.ds(pl.multiple_of(order_ref[j] * rows, rows), rows)
            to_ref[k, which] = grad_ref[at].astype(bf16)

    grad_ref[...] = dot(low_ref[...], gi_ref[...], 0, 0)
    spread(0)
    grad_ref[...] = dot(near_ref[...], act_ref[0:half], 0, 0) + dot(far_ref[...], act_ref[half:], 0, 0)
    spread(1)


def weight_grads(order, low, gi, near_half, far_half, act):
    n, d = low.shape
    hidden = act.shape[1]
    width = BLOCK
    parts = order.shape[0]
    sizes = (1,) if parts == 1 else (parts // 2, parts // 2)
    rows = d // parts
    wide = pl.BlockSpec((n, width), lambda i, order: (0, i))
    return pl.pallas_call(
        weight_grad_body,
        grid_spec=pltpu.PrefetchScalarGridSpec(
            num_scalar_prefetch=1,
            grid=(hidden // width,),
            in_specs=[fixed(n, d), wide, fixed(n // 2, d), fixed(n // 2, d), wide],
            out_specs=tuple(
                pl.BlockSpec((k, 2, rows, width), lambda i, order: (0, 0, 0, i)) for k in sizes
            ),
            scratch_shapes=[pltpu.VMEM((d, width), f32)],
        ),
        out_shape=tuple(out(k, 2, rows, hidden) for k in sizes),
        compiler_params=params(),
    )(order, low, gi, near_half, far_half, act)


def mix_back_body(where_ref, near_ref, far_ref, wo_ref, mix_ref, do_ref, pick_ref, gwo_ref):
    step = pl.program_id(0)
    half = pl.num_programs(0) // 2
    w, d = wo_ref.shape

    @pl.when(step == 0)
    def _():
        gwo_ref[...] = jnp.zeros_like(gwo_ref)

    row = lax.broadcasted_iota(jnp.int32, (w, d), 0) + where_ref[1] * w
    chosen = jnp.where(row == lax.broadcasted_iota(jnp.int32, (w, d), 1), 1.0, 0.0).astype(bf16)

    def run(from_ref):
        g = from_ref[...]
        do_ref[...] = dot(wo_ref[...], g, 1, 1).astype(bf16)
        pick_ref[...] = dot(chosen, g, 1, 1).astype(bf16)
        gwo_ref[...] += jnp.dot(mix_ref[...], g, preferred_element_type=f32)

    @pl.when(step < half)
    def _():
        run(near_ref)

    @pl.when(step >= half)
    def _():
        run(far_ref)


def mix_back(where, near_half, far_half, wo, mix):
    half, d = near_half.shape
    w = wo.shape[0]
    blocks = half // BLOCK
    columns = pl.BlockSpec((w, BLOCK), lambda i, where: (0, true_block(i, where, blocks)))
    return pl.pallas_call(
        mix_back_body,
        grid_spec=pltpu.PrefetchScalarGridSpec(
            num_scalar_prefetch=1,
            grid=(2 * blocks,),
            in_specs=[near((BLOCK, d), blocks), far((BLOCK, d), blocks), fixed(w, d), columns],
            out_specs=(columns, columns, fixed(w, d)),
        ),
        out_shape=(out(w, 2 * half), out(w, 2 * half), out(w, d, dtype=f32)),
        compiler_params=params(),
    )(where, near_half, far_half, wo, mix)


def project_grad_body(order_ref, dq_ref, dkv_ref, tok_ref, gwo_ref, bias_ref, *refs):
    *to_refs, grad_ref = refs
    w = dq_ref.shape[0]
    tok = tok_ref[...]
    grad_ref[0:w] = jnp.dot(dq_ref[...], tok, preferred_element_type=f32)
    grad_ref[w : 3 * w] = jnp.dot(dkv_ref[...], tok, preferred_element_type=f32)
    grad_ref[3 * w :] = gwo_ref[...]
    bias_ref[0:w] = jnp.sum(dq_ref[...].astype(f32), axis=1, keepdims=True)
    bias_ref[w:] = jnp.sum(dkv_ref[...].astype(f32), axis=1, keepdims=True)
    first = to_refs[0].shape[0]
    rows = to_refs[0].shape[1]
    for j in range(order_ref.shape[0]):
        to_ref, k = (to_refs[0], j) if j < first else (to_refs[1], j - first)
        at = pl.ds(pl.multiple_of(order_ref[j] * rows, rows), rows)
        to_ref[k] = grad_ref[at].astype(bf16)


def project_grads(order, dq, dkv, tok, gwo):
    w, n = dq.shape
    d = tok.shape[1]
    parts = order.shape[0]
    sizes = (1,) if parts == 1 else (parts // 2, parts // 2)
    return pl.pallas_call(
        project_grad_body,
        in_specs=[SMEM] + [VMEM] * 4,
        out_specs=(VMEM,) * (1 + len(sizes)),
        out_shape=(out(3 * w, 1, dtype=f32),) + tuple(out(k, 4 * w // parts, d) for k in sizes),
        scratch_shapes=[pltpu.VMEM((4 * w, d), f32)],
        compiler_params=params(),
    )(order, dq, dkv, tok, gwo)


def input_grad_body(share_ref, dq_ref, dkv_ref, wq_ref, wk_ref, wv_ref, here_ref, there_ref, all_ref):
    w = dq_ref.shape[0]
    part = dot(wq_ref[...], dq_ref[...], 0, 0)
    part = part + dot(wk_ref[...], dkv_ref[0:w], 0, 0)
    all_ref[...] = part + dot(wv_ref[...], dkv_ref[w:], 0, 0)
    for j in range(4):
        at = pl.ds(pl.multiple_of(share_ref[j] * w, w), w)
        to_ref = here_ref if j < 2 else there_ref
        to_ref[j % 2] = all_ref[at].astype(bf16)


def input_grads(shares, dq, dkv, wq, wk, wv):
    w, n = dq.shape
    d = wq.shape[1]
    width = 2 * BLOCK
    split = pl.BlockSpec((2, w, width), lambda i, shares: (0, 0, i))
    return pl.pallas_call(
        input_grad_body,
        grid_spec=pltpu.PrefetchScalarGridSpec(
            num_scalar_prefetch=1,
            grid=(n // width,),
            in_specs=[
                pl.BlockSpec((w, width), lambda i, shares: (0, i)),
                pl.BlockSpec((2 * w, width), lambda i, shares: (0, i)),
                fixed(w, d), fixed(w, d), fixed(w, d),
            ],
            out_specs=(split, split),
            scratch_shapes=[pltpu.VMEM((d, width), f32)],
        ),
        out_shape=(out(2, w, n), out(2, w, n)),
        compiler_params=params(),
    )(shares, dq, dkv, wq, wk, wv)


def settle_body(order_ref, near_ref, far_ref, q_ref, k_ref, v_ref, o_ref, all_ref):
    rows = near_ref.shape[1]
    first = near_ref.shape[0]
    for j in range(order_ref.shape[0]):
        from_ref, k = (near_ref, j) if j < first else (far_ref, j - first)
        at = pl.ds(pl.multiple_of(order_ref[j] * rows, rows), rows)
        all_ref[at] = from_ref[k].astype(f32)
    w = q_ref.shape[0]
    for k, to_ref in enumerate((q_ref, k_ref, v_ref, o_ref)):
        to_ref[...] = all_ref[k * w : (k + 1) * w]


def settle(order, near_part, far_part, w):
    d = near_part.shape[-1]
    return pl.pallas_call(
        settle_body,
        in_specs=[SMEM] + [VMEM] * 2,
        out_specs=(VMEM,) * 4,
        out_shape=(out(w, d, dtype=f32),) * 4,
        scratch_shapes=[pltpu.VMEM((4 * w, d), f32)],
        compiler_params=params(),
    )(order, near_part, far_part)


def halves_body(where_ref, near_ref, far_ref, to_ref):
    mine = pl.program_id(0) // (pl.num_programs(0) // 2) == where_ref[0]

    @pl.when(mine)
    def _():
        to_ref[...] = near_ref[...]

    @pl.when(jnp.logical_not(mine))
    def _():
        to_ref[...] = far_ref[...]


def halves(where, near_half, far_half):
    half, d = near_half.shape
    rows = half // 2
    take = pl.BlockSpec((rows, d), lambda i, where: (lax.rem(i, 2), 0))
    return pl.pallas_call(
        halves_body,
        grid_spec=pltpu.PrefetchScalarGridSpec(
            num_scalar_prefetch=1,
            grid=(4,),
            in_specs=[take, take],
            out_specs=pl.BlockSpec((rows, d), lambda i, where: (i, 0)),
        ),
        out_shape=out(2 * half, d),
        compiler_params=params(),
    )(where, near_half, far_half)


def swap(x, axis, bit):
    return lax.ppermute(x, axis, [(i, i ^ bit) for i in range(lax.axis_size(axis))])


def add_low(a, b):
    return (a.astype(f32) + b.astype(f32)).astype(bf16)


def shards(
    tokens, lengths, w_query, b_query, w_key, b_key, w_value, b_value, w_out, b_out, ln1_gain,
    ln1_bias, w_in, b_in, w_down, b_down, ln2_gain, ln2_bias, cotangent,
):
    dp = lax.axis_size("dp")
    n, d = tokens.shape
    w = w_query.shape[1]
    line = lambda v: v.reshape(1, -1)
    me = lax.axis_index("mp")
    core = me % 2
    where = jnp.stack([core, me]).astype(jnp.int32)
    wq, wk, wv = w_query.T, w_key.T, w_value.T

    stepwise = dp & (dp - 1) == 0 and dp > 1 and (d // dp) % 16 == 0
    bits = [1 << k for k in range(dp.bit_length() - 1)] if stepwise else []
    parts = 1 << len(bits)
    order = jnp.zeros((1,), jnp.int32)
    if stepwise:
        count = len(bits)
        places = [
            sum(bit for k, bit in enumerate(bits) if j >> (count - 1 - k) & 1) for j in range(parts)
        ]
        order = lax.axis_index("dp") ^ jnp.array(places, jnp.int32)

    def gather(own):
        held = own
        for bit in reversed(bits[1:]):
            held = jnp.concatenate([held, swap(held, "dp", bit)], axis=0)
        return held, swap(held, "dp", bits[0])

    def scatter_sum(keep, send):
        for k, bit in enumerate(bits):
            total = add_low(keep, swap(send, "dp", bit)) if k + 1 < len(bits) else (
                keep.astype(f32) + swap(send, "dp", bit).astype(f32)
            )
            keep, send = jnp.split(total, 2, axis=0) if k + 1 < len(bits) else (total, None)
        return keep

    if stepwise:
        w_near, w_far = gather(jnp.stack([w_in, w_down.T])[None])
    else:
        w_near = jnp.stack([
            lax.all_gather(w_in, "dp", axis=0, tiled=True),
            lax.all_gather(w_down.T, "dp", axis=0, tiled=True),
        ])[None]
        w_far = jnp.zeros((1, 2, 16, w_near.shape[-1]), bf16)
    wo_a = jnp.concatenate([w_out, swap(w_out, "mp", 2)], axis=0)
    wo_b = swap(wo_a, "mp", 1)

    qa, ka, va, cosine, sine = project(lengths, tokens, wq, wk, wv, b_query, b_key, b_value)
    p, mix, inv = attend(qa, ka, va)
    mix_a = jnp.concatenate([mix, swap(mix, "mp", 2)], axis=0)
    mix_b = swap(mix_a, "mp", 1)
    low, unit, scale, act, slope, own, other, wi, wd = feed_forward(
        where, order, mix_a, mix_b, wo_a, wo_b, tokens, line(b_out), line(ln1_gain), line(ln1_bias),
        w_near, w_far, line(b_in),
    )
    mine = add_low(own, swap(other, "mp", 1))
    theirs = swap(mine, "mp", 2)
    half_out, result_near, sums_two = second_norm(
        where, lengths, unit, line(ln1_gain), line(ln1_bias), mine, theirs, line(b_down),
        line(ln2_gain), line(ln2_bias), cotangent,
    )
    result_far = swap(result_near, "mp", 1)
    layer_out = halves(where, half_out, swap(half_out, "mp", 1))

    gi, own, other, sums_in = feed_back(result_near, result_far, wi, wd, slope)
    mine = add_low(own, swap(other, "mp", 1))
    theirs = swap(mine, "mp", 2)
    grads = weight_grads(order, low, gi, result_near, result_far, act)
    if stepwise:
        grads = scatter_sum(*grads)[0]
        grad_w_in, grad_w_down = grads[0], grads[1]
    else:
        grad_w_in, grad_w_down = (
            lax.psum_scatter(grads[0][0, k].astype(f32), "dp", scatter_dimension=0, tiled=True)
            for k in range(2)
        )
    near_half, sums_one = first_norm(unit, scale, line(ln1_gain), result_near, mine, theirs)
    far_half = swap(near_half, "mp", 1)
    do, pick, gwo = mix_back(where, near_half, far_half, w_out, mix)
    dq, dkv = attend_back(do, mix, inv, qa, ka, va, p, cosine, sine)

    shares = me ^ jnp.array([0, 2, 1, 3], jnp.int32)
    here, there = input_grads(shares, dq, dkv, wq, wk, wv)
    sum_here = here.astype(f32) + swap(there, "mp", 1).astype(f32)
    last = swap(sum_here[1].astype(bf16), "mp", 2)
    grad_tokens = sum_here[0] + last.astype(f32) + pick.astype(f32)

    bias, *pieces = project_grads(order, dq, dkv, tokens, gwo)
    norm_sums = jnp.concatenate([sums_one[0:3], sums_two[0:3]], axis=0)
    norm_sums = norm_sums + swap(norm_sums, "mp", 1)
    sums = jnp.concatenate([norm_sums, sums_in[0:1], jnp.pad(bias.reshape(1, -1), ((0, 0), (0, d - 3 * w)))])
    if stepwise:
        mine = scatter_sum(*pieces).astype(bf16)
        near_part, far_part = gather(mine)
        for bit in bits:
            sums = sums + swap(sums, "dp", bit)
    else:
        near_part = lax.psum(pieces[0].astype(f32), "dp").astype(bf16)
        far_part = jnp.zeros((1, 16, d), bf16)
        sums = lax.psum(sums, "dp")
    gq, gk, gv, go = settle(order, near_part, far_part, w)
    g1, s1, bo, g2, s2, bd, bi, qkv = (sums[k] for k in range(8))
    return (
        layer_out, grad_tokens.T, gq.T, qkv[0:w], gk.T, qkv[w : 2 * w], gv.T, qkv[2 * w : 3 * w],
        go, bo, g1, s1, grad_w_in, bi, grad_w_down.T, bd, g2, s2,
    )


def solution(mesh):
    in_specs = (
        P("dp", None), P("dp", None),
        P(None, "mp"), P("mp"), P(None, "mp"), P("mp"), P(None, "mp"), P("mp"),
        P("mp", None), P(), P(), P(),
        P("dp", "mp"), P("mp"), P("mp", "dp"), P(), P(), P(),
        P("dp", None),
    )
    out_specs = (
        P("dp", None), P("dp", "mp"),
        P(None, "mp"), P("mp"), P(None, "mp"), P("mp"), P(None, "mp"), P("mp"),
        P("mp", None), P(), P(), P(),
        P("dp", "mp"), P("mp"), P("mp", "dp"), P(), P(), P(),
    )
    return jax.shard_map(shards, mesh=mesh, in_specs=in_specs, out_specs=out_specs, check_vma=False)
```

```python
from functools import partial
import math

import jax
import jax.numpy as jnp
from jax import lax
from jax.experimental import pallas as pl
from jax.experimental.pallas import tpu as pltpu
from jax.sharding import PartitionSpec as P

HEAD_DIM = 64
HALF_DIM = HEAD_DIM // 2
WIDE = 128
USED = 80
MASKED = -1e30
LOG2E = math.log2(math.e)
EPS = 1e-12
BLOCK = 256
B_OUT, GAIN1, SHIFT1, B_IN, B_DOWN, GAIN2, SHIFT2 = (slice(k, k + 1) for k in range(7))
bf16 = jnp.bfloat16
f32 = jnp.float32
VMEM = pl.BlockSpec(memory_space=pltpu.VMEM)
SMEM = pl.BlockSpec(memory_space=pltpu.SMEM)
ANY = pl.BlockSpec(memory_space=pl.ANY)
HBM = pl.BlockSpec(memory_space=pltpu.HBM)
SHARE = 1e9


def launch(body, args, in_specs, out_shape, out_specs, *, mib, us, after=(), scalars=0, grid=(), scratch=()):
    taken, waits = len(args), len(after)

    def run(*refs):
        body(*refs[:taken], *refs[taken + waits :])

    return pl.pallas_call(
        run,
        grid_spec=pltpu.PrefetchScalarGridSpec(
            num_scalar_prefetch=scalars,
            grid=grid,
            in_specs=list(in_specs) + [ANY] * waits,
            out_specs=out_specs,
            scratch_shapes=list(scratch),
        ),
        out_shape=out_shape,
        compiler_params=pltpu.CompilerParams(vmem_limit_bytes=mib * 2**20),
        cost_estimate=pl.CostEstimate(flops=int(us * SHARE), bytes_accessed=0, transcendentals=0),
    )(*args, *after)


def out(*shape, dtype=bf16):
    return jax.ShapeDtypeStruct(shape, dtype)


def dot(left, right, left_dim, right_dim):
    return lax.dot_general(
        left, right, (((left_dim,), (right_dim,)), ((), ())), preferred_element_type=f32
    )


def qkv_body(
    len_ref, tok_ref, wq_ref, wk_ref, wv_ref, bq_ref, bk_ref, bv_ref, freq_ref,
    qa_ref, ka_ref, va_ref, cos_ref, sin_ref,
):
    n = tok_ref.shape[0]
    heads = wq_ref.shape[0] // HEAD_DIM
    pos = lax.broadcasted_iota(jnp.int32, (1, n), 1)
    first = len_ref[0, 0]
    used = first + len_ref[0, 1]
    in0, in1 = pos < first, pos < used
    start = jnp.where(in0, 0, jnp.where(in1, first, used))
    angles = freq_ref[...] * (pos - start).astype(f32)
    cosine, sine = jnp.cos(angles), jnp.sin(angles)
    cos_ref[...] = cosine
    sin_ref[...] = sine
    segment = jnp.where(in0, 0, jnp.where(in1, 1, 2))
    row = lax.broadcasted_iota(jnp.int32, (WIDE - HEAD_DIM, n), 0)
    same = row == segment
    q_tail = jnp.where(same, 1.0, 0.0).astype(bf16)
    k_tail = jnp.where(jnp.logical_or(same, row > 2), 0.0, MASKED).astype(bf16)
    v_tail = jnp.where(row < 3, 1.0, 0.0).astype(bf16)
    tok = tok_ref[...]

    def rotated(lin, h, scale):
        a = lin[h * HEAD_DIM : h * HEAD_DIM + HALF_DIM]
        b = lin[h * HEAD_DIM + HALF_DIM : (h + 1) * HEAD_DIM]
        x, y = a * cosine - b * sine, b * cosine + a * sine
        if scale != 1.0:
            x, y = x * scale, y * scale
        return x.astype(bf16), y.astype(bf16)

    for w_ref, b_ref, to_ref, tail, scale in (
        (wq_ref, bq_ref, qa_ref, q_tail, LOG2E / math.sqrt(HEAD_DIM)),
        (wk_ref, bk_ref, ka_ref, k_tail, 1.0),
        (wv_ref, bv_ref, va_ref, v_tail, None),
    ):
        column = jnp.broadcast_to(b_ref[...].reshape(1, -1), (8, b_ref.shape[0])).T[:, 0:1]
        lin = dot(w_ref[...], tok, 1, 1) + column
        for h in range(heads):
            if scale is None:
                to_ref[h, 0:HEAD_DIM] = lin[h * HEAD_DIM : (h + 1) * HEAD_DIM].astype(bf16)
            else:
                x, y = rotated(lin, h, scale)
                to_ref[h, 0:HALF_DIM] = x
                to_ref[h, HALF_DIM:HEAD_DIM] = y
            to_ref[h, HEAD_DIM:] = tail


def project(lengths, tok, wq, wk, wv, bq, bk, bv):
    n = tok.shape[0]
    heads = wq.shape[0] // HEAD_DIM
    freq = jnp.exp(jnp.arange(HALF_DIM, dtype=f32) * (-math.log(10000.0) / HALF_DIM))
    return launch(
        qkv_body, (lengths, tok, wq, wk, wv, bq, bk, bv, freq.reshape(-1, 1)),
        [SMEM] + [VMEM] * 8,
        (
            out(heads, WIDE, n), out(heads, WIDE, n), out(heads, WIDE, n),
            out(HALF_DIM, n, dtype=f32), out(HALF_DIM, n, dtype=f32),
        ),
        (VMEM,) * 5, mib=58, us=6,
    )


def chunk_block(chunk, half_blocks):
    first, count = chunk
    return lambda i: (i // count) * half_blocks + first + lax.rem(i, count)


def attend_body(qa_ref, ka_ref, va_ref, p_ref, mix_ref, inv_ref):
    heads, _, n = ka_ref.shape
    pieces = [slice(at, at + n // 3) for at in range(0, n, n // 3)]

    def score(h):
        scores = [dot(ka_ref[h, :, piece], qa_ref[h], 0, 0) for piece in pieces]
        top = jnp.max(scores[0], axis=0, keepdims=True)
        for s in scores[1:]:
            top = jnp.maximum(top, jnp.max(s, axis=0, keepdims=True))
        return scores, top

    def mix(h, scores, top):
        mixed = None
        for piece, s in zip(pieces, scores):
            p = jnp.exp2(s - top).astype(bf16)
            p_ref[h, piece] = p
            term = jnp.dot(va_ref[h, 0:USED, piece], p, preferred_element_type=f32)
            mixed = term if mixed is None else mixed + term
        inv = 1.0 / mixed[HEAD_DIM : HEAD_DIM + 1]
        mix_ref[h * HEAD_DIM : (h + 1) * HEAD_DIM] = (mixed[0:HEAD_DIM] * inv).astype(bf16)
        inv_ref[h] = inv

    following = score(0)
    for h in range(heads):
        current = following
        if h + 1 < heads:
            following = score(h + 1)
        mix(h, *current)


def attend(chunk, qa, ka, va, after=()):
    heads, _, n = qa.shape
    block = chunk_block(chunk, n // BLOCK // 2)
    steps = 2 * chunk[1]
    width = steps * BLOCK
    return launch(
        attend_body, (qa, ka, va),
        [pl.BlockSpec((heads, WIDE, BLOCK), lambda i: (0, 0, block(i))), VMEM, VMEM],
        (out(heads, n, width), out(heads * HEAD_DIM, width), out(heads, 1, width, dtype=f32)),
        (
            pl.BlockSpec((heads, n, BLOCK), lambda i: (0, 0, i)),
            pl.BlockSpec((heads * HEAD_DIM, BLOCK), lambda i: (0, i)),
            pl.BlockSpec((heads, 1, BLOCK), lambda i: (0, 0, i)),
        ),
        mib=56, us=2.4 * steps, grid=(steps,), after=after,
    )


def attend_back_body(
    last, do_ref, mix_ref, inv_ref, qa_ref, ka_ref, va_ref, p_ref, cos_ref, sin_ref, *refs
):
    if last:
        cos_all, sin_all, before, dq_ref, to_ref, dk_ref = refs
        held = ((dk_ref, before),)
    else:
        *before, dq_ref, dk_ref, dv_ref = refs
        held = tuple(zip((dk_ref, dv_ref), before or (None, None)))
    heads, _, width = qa_ref.shape
    n = ka_ref.shape[2]
    pieces = [slice(at, at + n // 3) for at in range(0, n, n // 3)]

    @pl.when(pl.program_id(0) == 0)
    def _():
        for acc, start in held:
            acc[...] = jnp.zeros_like(acc) if start is None else start[...]

    def score_grad(h):
        rows = slice(h * HEAD_DIM, (h + 1) * HEAD_DIM)
        do = (do_ref[rows].astype(f32) * inv_ref[h]).astype(bf16)
        delta = jnp.sum(do.astype(f32) * mix_ref[rows].astype(f32), axis=0, keepdims=True)
        d1 = delta.astype(bf16).astype(f32)
        d2 = (delta - d1).astype(bf16).astype(f32)
        d3 = delta - d1 - d2
        row = lax.broadcasted_iota(jnp.int32, (USED - HEAD_DIM, width), 0)
        tail = jnp.where(row == 0, -d1, jnp.where(row == 1, -d2, jnp.where(row == 2, -d3, 0.0)))
        do_wide = jnp.concatenate([do, tail.astype(bf16)], axis=0)
        return do, [dot(va_ref[h, 0:USED, piece], do_wide, 0, 0) for piece in pieces]

    def finish(h, do, grads):
        lo, mid, hi = h * HEAD_DIM, h * HEAD_DIM + HALF_DIM, (h + 1) * HEAD_DIM
        dq = None
        for piece, dp in zip(pieces, grads):
            p = p_ref[h, piece]
            ds = (p.astype(f32) * dp).astype(bf16)
            term = jnp.dot(ka_ref[h, 0:HEAD_DIM, piece], ds, preferred_element_type=f32)
            dq = term if dq is None else dq + term
            dk_ref[lo:hi, piece] += dot(qa_ref[h, 0:HEAD_DIM], ds, 1, 1)
            if not last:
                dv_ref[lo:hi, piece] += dot(do, p, 1, 1)
        dq = dq * (1.0 / math.sqrt(HEAD_DIM))
        dq_ref[lo:mid], dq_ref[mid:hi] = turned_back(
            dq[0:HALF_DIM], dq[HALF_DIM:HEAD_DIM], cos_ref[...], sin_ref[...]
        )

    following = score_grad(0)
    for h in range(heads):
        current = following
        if h + 1 < heads:
            following = score_grad(h + 1)
        finish(h, *current)
    if last:

        @pl.when(pl.program_id(0) == pl.num_programs(0) - 1)
        def _():
            for lo in range(0, dk_ref.shape[0], HEAD_DIM):
                mid, hi = lo + HALF_DIM, lo + HEAD_DIM
                a, b = dk_ref[lo:mid] * math.log(2.0), dk_ref[mid:hi] * math.log(2.0)
                to_ref[lo:mid], to_ref[mid:hi] = turned_back(a, b, cos_all[...], sin_all[...])


def turned_back(a, b, cosine, sine):
    return (a * cosine + b * sine).astype(bf16), (b * cosine - a * sine).astype(bf16)


def attend_back(chunk, do, mix, inv, qa, ka, va, p, cosine, sine, before, last, after=()):
    heads, _, n = qa.shape
    w = heads * HEAD_DIM
    block = chunk_block(chunk, n // BLOCK // 2)
    steps = 2 * chunk[1]
    columns = pl.BlockSpec((w, BLOCK), lambda i: (0, i))
    table = pl.BlockSpec((HALF_DIM, BLOCK), lambda i: (0, block(i)))
    before = (cosine, sine, *before) if last else before
    shapes = (out(w, steps * BLOCK), out(w, n)) if last else (
        out(w, steps * BLOCK), out(w, n, dtype=f32), out(w, n, dtype=f32)
    )
    return launch(
        partial(attend_back_body, last),
        (do, mix, inv, qa, ka, va, p, cosine, sine, *before),
        [
            columns,
            columns,
            pl.BlockSpec((heads, 1, BLOCK), lambda i: (0, 0, i)),
            pl.BlockSpec((heads, WIDE, BLOCK), lambda i: (0, 0, block(i))),
            VMEM,
            VMEM,
            pl.BlockSpec((heads, n, BLOCK), lambda i: (0, 0, i)),
            table,
            table,
        ] + [VMEM] * len(before),
        shapes, (columns,) + (VMEM,) * (len(shapes) - 1),
        mib=32, us=3 * steps, grid=(steps,), after=after,
        scratch=[pltpu.VMEM((w, n), f32)] if last else (),
    )


def value_grad_body(do_ref, inv_ref, p_ref, before, to_ref, acc):
    step = pl.program_id(0)

    @pl.when(step == 0)
    def _():
        acc[...] = before[...]

    for h in range(p_ref.shape[0]):
        rows = slice(h * HEAD_DIM, (h + 1) * HEAD_DIM)
        do = (do_ref[rows].astype(f32) * inv_ref[h]).astype(bf16)
        acc[rows] += dot(do, p_ref[h], 1, 1)

    @pl.when(step == pl.num_programs(0) - 1)
    def _():
        to_ref[...] = acc[...].astype(bf16)


def value_grad(do, inv, p, before, after=()):
    heads, n, width = p.shape
    w = heads * HEAD_DIM
    return launch(
        value_grad_body, (do, inv, p, before),
        [
            pl.BlockSpec((w, BLOCK), lambda i: (0, i)),
            pl.BlockSpec((heads, 1, BLOCK), lambda i: (0, 0, i)),
            pl.BlockSpec((heads, n, BLOCK), lambda i: (0, 0, i)),
            VMEM,
        ],
        out(w, n), VMEM, mib=20, us=2, grid=(width // BLOCK,), after=after,
        scratch=[pltpu.VMEM((w, n), f32)],
    )


def by_core(chunk, half_blocks, other):
    first, _ = chunk

    def index(i, where):
        return lax.rem(where[0] + other, 2) * half_blocks + first + i

    return index


def by_run(chunk, other):
    return lambda i, where: lax.rem(where[0] + other, 2) * chunk[1] + i


def assemble(order, pieces, which, after=()):
    rows, d = pieces[0].shape[2:]
    count, parts = len(pieces), sum(piece.shape[0] for piece in pieces)

    def body(order_ref, *refs):
        to_ref = refs[count]
        held = [(ref, k) for ref in refs[0:count] for k in range(ref.shape[0])]
        for j, (ref, k) in enumerate(held):
            to_ref[pl.ds(pl.multiple_of(order_ref[j] * rows, rows), rows)] = ref[k, which]

    return launch(
        body, (order, *pieces), [SMEM] + [VMEM] * count, out(parts * rows, d), VMEM,
        mib=12, us=0.6, after=after,
    )


def add_body(a_ref, b_ref, to_ref):
    to_ref[...] = (a_ref[...].astype(f32) + b_ref[...].astype(f32)).astype(bf16)


def add_low(a, b, after=()):
    return launch(
        add_body, (a, b), [VMEM] * 2, out(*a.shape), VMEM, mib=8, us=0.5, after=after
    )


def join_body(a_ref, b_ref, to_ref):
    k = a_ref.shape[0]
    to_ref[0:k] = a_ref[...]
    to_ref[k:] = b_ref[...]


def join(a, b, after=()):
    return launch(
        join_body, (a, b), [VMEM, VMEM], out(a.shape[0] + b.shape[0], *a.shape[1:]), VMEM,
        mib=8, us=0.5, after=after,
    )


def forward_body(*refs):
    where_ref, *refs = refs
    mixes, outs = refs[0:8], refs[8:12]
    (tok_own, tok_other, vec_ref, wi_ref, wd_ref,
     low_ref, unit_ref, scale_ref, act_ref, slope_ref, own_ref, other_ref) = refs[12:]

    def norm(k):
        z = (tok_own, tok_other)[k][...].astype(f32) + vec_ref[B_OUT]
        for mix_ref, wo_ref in zip(mixes[k::2], outs):
            z = z + dot(mix_ref[...], wo_ref[...], 0, 0)
        center = z - jnp.mean(z, axis=-1, keepdims=True)
        scale = lax.rsqrt(jnp.mean(center * center, axis=-1, keepdims=True) + EPS)
        unit = center * scale
        low = (unit * vec_ref[GAIN1] + vec_ref[SHIFT1]).astype(bf16)
        low_ref[k] = low
        if k == 0:
            unit_ref[...] = unit.astype(bf16)
            scale_ref[...] = scale
        return low

    def expand(k, low):
        return jnp.dot(low, wi_ref[...], preferred_element_type=f32) + vec_ref[B_IN]

    def activate(k, inner):
        phi = 0.5 * lax.erf(inner * math.sqrt(0.5)) + 0.5
        bell = jnp.exp2(inner * inner * (-0.5 * LOG2E)) * (1.0 / math.sqrt(2.0 * math.pi))
        act = (inner * phi).astype(bf16)
        act_ref[k] = act
        slope_ref[k] = (phi + inner * bell).astype(bf16)
        return act

    def contract(k, act):
        (own_ref, other_ref)[k][...] = dot(act, wd_ref[...], 1, 1).astype(bf16)

    low_b = norm(1)
    inner_b = expand(1, low_b)
    low_a = norm(0)
    act_b = activate(1, inner_b)
    inner_a = expand(0, low_a)
    contract(1, act_b)
    contract(0, activate(0, inner_a))


def feed_forward(chunk, where, mixes, outs, tok, vec, wi, wd, after=()):
    n, d = tok.shape
    hidden = wi.shape[1]
    half_blocks = n // BLOCK // 2
    count = chunk[1]
    rows = count * BLOCK
    w = mixes[0].shape[0]
    own_run, other_run = by_run(chunk, 0), by_run(chunk, 1)
    own_block, other_block = by_core(chunk, half_blocks, 0), by_core(chunk, half_blocks, 1)
    mix_specs, mix_args = [], []
    for m in mixes:
        mix_specs += [
            pl.BlockSpec((w, BLOCK), lambda i, where: (0, own_run(i, where))),
            pl.BlockSpec((w, BLOCK), lambda i, where: (0, other_run(i, where))),
        ]
        mix_args += [m, m]
    both = lambda width: pl.BlockSpec((2, BLOCK, width), lambda i, where: (0, i, 0))
    one = lambda width: pl.BlockSpec((BLOCK, width), lambda i, where: (i, 0))
    return launch(
        forward_body, (where, *mix_args, *outs, tok, tok, vec, wi, wd),
        mix_specs + [VMEM] * 4 + [
            pl.BlockSpec((BLOCK, d), lambda i, where: (own_block(i, where), 0)),
            pl.BlockSpec((BLOCK, d), lambda i, where: (other_block(i, where), 0)),
        ] + [VMEM] * 3,
        (
            out(2, rows, d), out(rows, d), out(rows, 1, dtype=f32), out(2, rows, hidden),
            out(2, rows, hidden), out(rows, d), out(rows, d),
        ),
        (both(d), one(d), one(1), both(hidden), both(hidden), one(d), one(d)),
        mib=24, us=4.5 * count, scalars=1, grid=(count,), after=after,
    )


def norm_back(g, unit, scale, gain):
    q = g * gain
    return scale * (
        q - jnp.mean(q, axis=-1, keepdims=True) - unit * jnp.mean(q * unit, axis=-1, keepdims=True)
    )


def put_sums(sums_ref, *terms):
    sums_ref[...] = jnp.zeros_like(sums_ref)
    for k, term in enumerate(terms):
        sums_ref[k : k + 1] = jnp.sum(term, axis=0, keepdims=True)


def second_norm_body(
    first, where_ref, len_ref, unit_ref, mine_ref, theirs_ref, vec_ref, cot_ref,
    out_ref, low_ref, sums_ref, held, sem,
):
    rows = unit_ref.shape[0]
    half = cot_ref.shape[0] // 2
    start = pl.multiple_of(where_ref[0] * half + first, BLOCK)
    copy = pltpu.make_async_copy(cot_ref.at[pl.ds(start, rows)], held, sem)
    copy.start()
    total = mine_ref[...].astype(f32) + theirs_ref[...].astype(f32)
    z = unit_ref[...].astype(f32) * vec_ref[GAIN1] + vec_ref[SHIFT1] + total + vec_ref[B_DOWN]
    center = z - jnp.mean(z, axis=-1, keepdims=True)
    scale = lax.rsqrt(jnp.mean(center * center, axis=-1, keepdims=True) + EPS)
    unit = center * scale
    out_ref[...] = (unit * vec_ref[GAIN2] + vec_ref[SHIFT2]).astype(bf16)
    slot = start + lax.broadcasted_iota(jnp.int32, (rows, 1), 0)
    copy.wait()
    g = jnp.where(slot < len_ref[0, 0] + len_ref[0, 1], held[...], 0.0)
    back = norm_back(g, unit, scale, vec_ref[GAIN2])
    low_ref[...] = back.astype(bf16)
    put_sums(sums_ref, g * unit, g, back)


def second_norm(chunk, where, lengths, unit, mine, theirs, vec, cot, after=()):
    rows, d = unit.shape
    return launch(
        partial(second_norm_body, chunk[0] * BLOCK),
        (where, lengths, unit, mine, theirs, vec, cot), [SMEM] * 2 + [VMEM] * 4 + [HBM],
        (out(rows, d), out(rows, d), out(8, d, dtype=f32)), (VMEM,) * 3,
        mib=12, us=2, after=after,
        scratch=[pltpu.VMEM((rows, d), f32), pltpu.SemaphoreType.DMA(())],
    )


def first_norm_body(unit_ref, scale_ref, vec_ref, skip_ref, mine_ref, theirs_ref, low_ref, sums_ref):
    g = skip_ref[...].astype(f32) + (mine_ref[...].astype(f32) + theirs_ref[...].astype(f32))
    unit = unit_ref[...].astype(f32)
    back = norm_back(g, unit, scale_ref[...], vec_ref[GAIN1])
    low_ref[...] = back.astype(bf16)
    put_sums(sums_ref, g * unit, g, back)


def first_norm(unit, scale, vec, skip, mine, theirs, after=()):
    rows, d = skip.shape
    return launch(
        first_norm_body, (unit, scale, vec, skip, mine, theirs), [VMEM] * 6,
        (out(rows, d), out(8, d, dtype=f32)), (VMEM,) * 2, mib=12, us=1, after=after,
    )


def backward_body(near_ref, far_ref, wi_ref, wd_ref, slope_ref, gi_ref, own_ref, other_ref, sums_ref):
    def open_up(k):
        return jnp.dot((near_ref, far_ref)[k][...], wd_ref[...], preferred_element_type=f32)

    def slopes(k, g):
        g = (g * slope_ref[k].astype(f32)).astype(bf16)
        gi_ref[k] = g
        return g

    def close(k, g):
        (own_ref, other_ref)[k][...] = dot(g, wi_ref[...], 1, 1).astype(bf16)

    open_b = open_up(1)
    open_a = open_up(0)
    g_b = slopes(1, open_b)
    close(1, g_b)
    g_a = slopes(0, open_a)
    close(0, g_a)
    put_sums(sums_ref, g_a.astype(f32) + g_b.astype(f32))


def feed_back(near_low, far_low, wi, wd, slope, after=()):
    rows, d = near_low.shape
    hidden = slope.shape[2]
    return launch(
        backward_body, (near_low, far_low, wi, wd, slope), [VMEM] * 5,
        (out(2, rows, hidden), out(rows, d), out(rows, d), out(8, hidden, dtype=f32)),
        (VMEM,) * 4, mib=12, us=1.6, after=after,
    )


def weight_grad_body(order_ref, *refs):
    chunks = (len(refs) - 2) // 5 if len(refs) % 5 == 2 else (len(refs) - 3) // 5
    lows, gis, acts = refs[0:chunks], refs[chunks : 2 * chunks], refs[2 * chunks : 3 * chunks]
    nears, fars = refs[3 * chunks : 4 * chunks], refs[4 * chunks : 5 * chunks]
    *to_refs, grad_ref = refs[5 * chunks :]

    def spread(which):
        first = to_refs[0].shape[0]
        rows = to_refs[0].shape[2]
        for j in range(order_ref.shape[0]):
            to_ref, k = (to_refs[0], j) if j < first else (to_refs[1], j - first)
            at = pl.ds(pl.multiple_of(order_ref[j] * rows, rows), rows)
            to_ref[k, which] = grad_ref[at].astype(bf16)

    total = None
    for low_ref, gi_ref in zip(lows, gis):
        for k in range(2):
            term = dot(low_ref[k], gi_ref[k], 0, 0)
            total = term if total is None else total + term
    grad_ref[...] = total
    spread(0)
    total = None
    for near_ref, far_ref, act_ref in zip(nears, fars, acts):
        term = dot(near_ref[...], act_ref[0], 0, 0) + dot(far_ref[...], act_ref[1], 0, 0)
        total = term if total is None else total + term
    grad_ref[...] = total
    spread(1)


def weight_grads(order, lows, gis, acts, nears, fars, after=()):
    d, hidden = lows[0].shape[2], gis[0].shape[2]
    width = BLOCK
    parts = order.shape[0]
    sizes = (1,) if parts == 1 else (parts // 2, parts // 2)
    rows = d // parts
    wide = [pl.BlockSpec((2, a.shape[1], width), lambda i, order: (0, 0, i)) for a in gis]
    return launch(
        weight_grad_body, (order, *lows, *gis, *acts, *nears, *fars),
        [VMEM] * len(lows) + wide + wide + [VMEM] * (2 * len(lows)),
        tuple(out(k, 2, rows, hidden) for k in sizes),
        tuple(pl.BlockSpec((k, 2, rows, width), lambda i, order: (0, 0, 0, i)) for k in sizes),
        mib=20, us=6, scalars=1, grid=(hidden // width,),
        scratch=[pltpu.VMEM((d, width), f32)], after=after,
    )


def mix_back_body(where_ref, near_ref, far_ref, wo_ref, mix_ref, do_ref, pick_ref, gwo_ref):
    w, d = wo_ref.shape

    @pl.when(pl.program_id(0) == 0)
    def _():
        gwo_ref[...] = jnp.zeros_like(gwo_ref)

    row = lax.broadcasted_iota(jnp.int32, (w, d), 0) + where_ref[1] * w
    chosen = jnp.where(row == lax.broadcasted_iota(jnp.int32, (w, d), 1), 1.0, 0.0).astype(bf16)

    def run(from_ref):
        g = from_ref[...]
        do_ref[...] = dot(wo_ref[...], g, 1, 1).astype(bf16)
        pick_ref[...] = dot(chosen, g, 1, 1).astype(bf16)
        gwo_ref[...] += jnp.dot(mix_ref[...], g, preferred_element_type=f32)

    @pl.when(pl.program_id(0) == where_ref[0])
    def _():
        run(near_ref)

    @pl.when(pl.program_id(0) != where_ref[0])
    def _():
        run(far_ref)


def mix_back(where, near_half, far_half, wo, mix, after=()):
    rows, d = near_half.shape
    w = wo.shape[0]
    columns = pl.BlockSpec((w, rows), lambda i, where: (0, i))
    return launch(
        mix_back_body, (where, near_half, far_half, wo, mix), [VMEM, VMEM, VMEM, columns],
        (out(w, 2 * rows), out(w, 2 * rows), out(w, d, dtype=f32)),
        (columns, columns, pl.BlockSpec((w, d), lambda i, where: (0, 0))),
        mib=12, us=2, scalars=1, grid=(2,), after=after,
    )


def slot_runs(chunks, n):
    return [(first * BLOCK, n // 2 + first * BLOCK, count * BLOCK) for first, count in chunks]


def spread(order_ref, grad_ref, to_refs, rows):
    first = to_refs[0].shape[0]
    for j in range(order_ref.shape[0]):
        to_ref, k = (to_refs[0], j) if j < first else (to_refs[1], j - first)
        at = pl.ds(pl.multiple_of(order_ref[j] * rows, rows), rows)
        to_ref[k, 0:rows] = grad_ref[at].astype(bf16)


def total(refs):
    result = refs[0][...]
    for ref in refs[1:]:
        result = result + ref[...]
    return result


def split_parts(order):
    parts = order.shape[0]
    return (1,) if parts == 1 else (parts // 2, parts // 2)


def value_project(order, dv, tok, gwos, after=()):
    w, d = gwos[0].shape
    sizes = split_parts(order)
    count = len(gwos)

    def body(order_ref, dv_ref, tok_ref, *refs):
        *to_refs, grad_ref = refs[count:]
        grad_ref[0:w] = jnp.dot(dv_ref[...], tok_ref[...], preferred_element_type=f32)
        grad_ref[w:] = total(refs[0:count])
        spread(order_ref, grad_ref, to_refs, 2 * w // order_ref.shape[0])

    return launch(
        body, (order, dv, tok, *gwos), [SMEM] + [VMEM] * (2 + count),
        tuple(out(k, 2 * w // sum(sizes), d) for k in sizes), (VMEM,) * len(sizes),
        mib=16, us=1.5, scratch=[pltpu.VMEM((2 * w, d), f32)], after=after,
    )


def key_project(chunks, order, dqs, dk, dv, tok, sums, far_sums, after=()):
    w, n = dk.shape
    d = tok.shape[1]
    sizes = split_parts(order)
    count = len(dqs)
    parts = sum(sizes)
    rows = 2 * w // parts
    runs = slot_runs(chunks, n)

    def body(order_ref, dk_ref, dv_ref, tok_ref, sums_ref, far_ref, *refs):
        dq_refs, (*to_refs, grad_ref, vec_ref) = refs[0:count], refs[count:]
        ones = jnp.ones((8, n), bf16)
        grad = row = None
        for dq_ref, (first, second, length) in zip(dq_refs, runs):
            bias = dot(ones[:, 0 : 2 * length], dq_ref[...], 1, 1)
            row = bias if row is None else row + bias
            for k, at in enumerate((first, second)):
                term = jnp.dot(
                    dq_ref[:, k * length : (k + 1) * length], tok_ref[at : at + length],
                    preferred_element_type=f32,
                )
                grad = term if grad is None else grad + term
        grad_ref[0:w] = grad
        grad_ref[w:] = jnp.dot(dk_ref[...], tok_ref[...], preferred_element_type=f32)
        vec_ref[...] = sums_ref[...]
        vec_ref[0:6] = sums_ref[0:6] + far_ref[0:6]
        biases = [row, dot(ones, dk_ref[...], 1, 1), dot(ones, dv_ref[...], 1, 1)]
        biases.append(jnp.zeros((8, d - 3 * w), f32))
        vec_ref[7:8] = jnp.concatenate(biases, axis=1)[0:1]
        spread(order_ref, grad_ref, to_refs, rows)
        for j in range(parts):
            to_ref, k = (to_refs[0], j) if j < sizes[0] else (to_refs[1], j - sizes[0])
            tail = vec_ref[...] if parts == 1 else jnp.broadcast_to(
                vec_ref[pl.ds(order_ref[j], 1)], (8, d)
            )
            to_ref[k, rows:] = jnp.concatenate([tail, tail], axis=0).astype(bf16)

    return launch(
        body, (order, dk, dv, tok, sums, far_sums, *dqs), [SMEM] + [VMEM] * (5 + count),
        tuple(out(k, rows + 16, d) for k in sizes), (VMEM,) * len(sizes),
        mib=16, us=2, after=after,
        scratch=[pltpu.VMEM((2 * w, d), f32), pltpu.VMEM((8, d), f32)],
    )


def add_sums(ones, twos, ins, after=()):
    count = len(ones)

    def body(*refs):
        to_ref = refs[-1]
        to_ref[...] = jnp.zeros_like(to_ref)
        to_ref[0:3] = total([ref for ref in refs[0:count]])[0:3]
        to_ref[3:6] = total([ref for ref in refs[count : 2 * count]])[0:3]
        to_ref[6:7] = total([ref for ref in refs[2 * count : 3 * count]])[0:1]

    return launch(
        body, (*ones, *twos, *ins), [VMEM] * (3 * count), out(*ones[0].shape, dtype=f32), VMEM,
        mib=4, us=0.5, after=after,
    )


def input_grad_body(runs, share_ref, dk_ref, dv_ref, wq_ref, wk_ref, wv_ref, *refs):
    *dqs, here_ref, there_ref, all_ref = refs
    w = dk_ref.shape[0]
    for dq_ref, (first, second, length) in zip(dqs, runs):
        for k, at in enumerate((first, second)):
            slots = slice(at, at + length)
            part = dot(wq_ref[...], dq_ref[:, k * length : (k + 1) * length], 0, 0)
            part = part + dot(wk_ref[...], dk_ref[:, slots], 0, 0)
            all_ref[:, slots] = part + dot(wv_ref[...], dv_ref[:, slots], 0, 0)
    for j in range(4):
        at = pl.ds(pl.multiple_of(share_ref[j] * w, w), w)
        to_ref = here_ref if j < 2 else there_ref
        to_ref[j % 2] = all_ref[at].astype(bf16)


def input_grads(chunks, shares, dqs, dk, dv, wq, wk, wv, after=()):
    w, d = wq.shape
    n = dk.shape[1]
    return launch(
        partial(input_grad_body, slot_runs(chunks, n)), (shares, dk, dv, wq, wk, wv, *dqs),
        [SMEM] + [VMEM] * (5 + len(chunks)), (out(2, w, n), out(2, w, n)), (VMEM, VMEM),
        mib=20, us=3, scratch=[pltpu.VMEM((d, n), f32)], after=after,
    )


def token_grad_body(runs, here_ref, there_ref, *refs):
    *picks, send_ref, keep_ref = refs
    send_ref[...] = (here_ref[1].astype(f32) + there_ref[1].astype(f32)).astype(bf16)
    for pick_ref, (first, second, length) in zip(picks, runs):
        for k, at in enumerate((first, second)):
            slots = slice(at, at + length)
            keep_ref[:, slots] = (
                here_ref[0, :, slots].astype(f32) + there_ref[0, :, slots].astype(f32)
                + pick_ref[:, k * length : (k + 1) * length].astype(f32)
            )


def token_grads(chunks, here, there, picks, after=()):
    _, w, n = here.shape
    return launch(
        partial(token_grad_body, slot_runs(chunks, n)), (here, there, *picks),
        [VMEM] * (2 + len(chunks)), (out(w, n), out(w, n, dtype=f32)), (VMEM, VMEM),
        mib=12, us=1.5, after=after,
    )


def settle(order, pieces, w, sums=False, after=()):
    d = pieces[0].shape[-1]
    count, parts = len(pieces), order.shape[0]
    rows = 2 * w // parts

    def body(order_ref, *refs):
        from_refs, to_refs, all_ref = refs[0:count], refs[count:-1], refs[-1]
        held = [(ref, k) for ref in from_refs for k in range(ref.shape[0])]
        for j, (ref, k) in enumerate(held):
            at = pl.ds(pl.multiple_of(order_ref[j] * rows, rows), rows)
            all_ref[at] = ref[k, 0:rows].astype(f32)
            if sums:
                tail = ref[k, rows:].astype(f32)
                if parts == 1:
                    to_refs[2][...] = tail[0:8]
                else:
                    to_refs[2][pl.ds(order_ref[j], 1)] = tail[0:1]
        to_refs[0][...] = all_ref[0:w]
        to_refs[1][...] = all_ref[w:]

    shapes = (out(w, d, dtype=f32),) * 2 + ((out(8, d, dtype=f32),) if sums else ())
    return launch(
        body, (order, *pieces), [SMEM] + [VMEM] * count, shapes, (VMEM,) * len(shapes),
        mib=12, us=1, scratch=[pltpu.VMEM((2 * w, d), f32)], after=after,
    )


def place_body(runs, where_ref, *refs):
    count = len(runs)
    nears, fars, to_ref = refs[0:count], refs[count : 2 * count], refs[-1]
    core = where_ref[0]
    half = to_ref.shape[0] // 2
    for near_ref, far_ref, (first, _, length) in zip(nears, fars, runs):
        for ref, owner in ((near_ref, core), (far_ref, 1 - core)):
            at = pl.ds(pl.multiple_of(owner * half + first, BLOCK), length)
            to_ref[at] = ref[...]


def place(chunks, where, nears, fars, n, after=()):
    d = nears[0].shape[1]
    return launch(
        partial(place_body, slot_runs(chunks, n)), (where, *nears, *fars),
        [SMEM] + [VMEM] * (2 * len(chunks)), out(n, d), VMEM, mib=12, us=2, after=after,
    )


def swap(x, axis, bit):
    return lax.ppermute(x, axis, [(i, i ^ bit) for i in range(lax.axis_size(axis))])


def split_slots(n):
    half_blocks = n // BLOCK // 2
    return [(k, 1) for k in range(half_blocks)]


def shards(
    tokens, lengths, w_query, b_query, w_key, b_key, w_value, b_value, w_out, b_out, ln1_gain,
    ln1_bias, w_in, b_in, w_down, b_down, ln2_gain, ln2_bias, cotangent,
):
    dp = lax.axis_size("dp")
    n, d = tokens.shape
    w = w_query.shape[1]
    chunks = split_slots(n)
    me = lax.axis_index("mp")
    core = me % 2
    where = jnp.stack([core, me]).astype(jnp.int32)
    wq, wk, wv = w_query.T, w_key.T, w_value.T

    stepwise = dp & (dp - 1) == 0 and dp > 1 and (d // dp) % 16 == 0
    bits = [1 << k for k in range(dp.bit_length() - 1)] if stepwise else []
    parts = 1 << len(bits)
    order = jnp.zeros((1,), jnp.int32)
    if stepwise:
        count = len(bits)
        places = [
            sum(bit for k, bit in enumerate(bits) if j >> (count - 1 - k) & 1) for j in range(parts)
        ]
        order = lax.axis_index("dp") ^ jnp.array(places, jnp.int32)

    def gather(own):
        held = own
        for bit in reversed(bits[1:]):
            held = join(held, swap(held, "dp", bit))
        return held, swap(held, "dp", bits[0])

    def scatter_sum(keep, send):
        for k, bit in enumerate(bits):
            total = keep.astype(f32) + swap(send, "dp", bit).astype(f32)
            if k + 1 < len(bits):
                keep, send = jnp.split(total.astype(bf16), 2, axis=0)
        return total

    vec = jnp.stack([b_out, ln1_gain, ln1_bias, b_in, b_down, ln2_gain, ln2_bias, b_down])
    qa, ka, va, cosine, sine = project(lengths, tokens, wq, wk, wv, b_query, b_key, b_value)
    out_y = swap(w_out, "mp", 2)
    outs = (w_out, out_y, swap(w_out, "mp", 1), swap(out_y, "mp", 1))

    each, last = range(len(chunks)), len(chunks) - 1
    kept, mixes = [], []

    def run_attend(k, *after):
        kept.append(attend(chunks[k], qa, ka, va, after))
        mix = kept[k][1]
        mix_y = swap(mix, "mp", 2)
        mixes.append((mix, mix_y, swap(mix, "mp", 1), swap(mix_y, "mp", 1)))
        return kept[k][2]

    both = jnp.stack([w_in, w_down.T])[None]
    if stepwise:
        near, far = [both], [swap(both, "dp", bits[0])]
        held, got = both, []
        for k in each:
            if 0 < k < len(bits):
                came = swap(held, "dp", bits[-k])
                near.append(came)
                far.append(swap(came, "dp", bits[0]))
                got = far[k - 1 : k]
                if k + 1 < len(bits):
                    held = join(held, came, (ready,))
                    got.append(held)
                else:
                    got.append(came)
            ready = run_attend(k, ready if k else cosine, *got)
            got = []
        gathered = near + far
    else:
        for k in each:
            ready = run_attend(k, ready if k else cosine)
        gathered = [jnp.stack([
            lax.all_gather(part, "dp", axis=0, tiled=True) for part in (w_in, w_down.T)
        ])[None]]
    wi, wd = (assemble(order, gathered, k, (ready,)) for k in range(2))

    made = {}

    def run(name, k, *waits):
        nonlocal ready
        after = (ready, *waits)
        if name == "forward":
            made[name, k] = feed_forward(
                chunks[k], where, mixes[k], outs, tokens, vec, wi, wd, after
            )
            ready = made[name, k][2]
        elif name == "sum two":
            *_, own, other = made["forward", k]
            mine = ready = add_low(own, swap(other, "mp", 1), after)
            made[name, k] = mine, swap(mine, "mp", 2)
        elif name == "norm two":
            made[name, k] = second_norm(
                chunks[k], where, lengths, made["forward", k][1], *made["sum two", k], vec,
                cotangent, after,
            )
            made["low", k] = made[name, k][1], swap(made[name, k][1], "mp", 1)
            ready = made[name, k][2]
        elif name == "back":
            made[name, k] = feed_back(*made["low", k], wi, wd, made["forward", k][4], after)
            ready = made[name, k][3]
        elif name == "sum one":
            _, own, other, _ = made["back", k]
            mine = ready = add_low(own, swap(other, "mp", 1), after)
            made[name, k] = mine, swap(mine, "mp", 2)
        elif name == "weights":
            forwards = [made["forward", c] for c in range(len(chunks))]
            nears, fars = zip(*(made["low", c] for c in range(len(chunks))))
            made[name] = weight_grads(
                order, [f[0] for f in forwards], [made["back", c][0] for c in range(len(chunks))],
                [f[3] for f in forwards], nears, fars, after,
            )
            ready = made[name][0]
        elif name == "norm one":
            forward = made["forward", k]
            half, sums = first_norm(
                forward[1], forward[2], vec, made["low", k][0], *made["sum one", k], after
            )
            made[name, k] = half, swap(half, "mp", 1), sums
            ready = sums
        elif name == "mix":
            made[name, k] = mix_back(where, *made["norm one", k][0:2], w_out, kept[k][1], after)
            ready = made[name, k][0]
        elif name == "attend":
            p, mix, inv = kept[k]
            before = made[name, k - 1][1:] if k else ()
            if k == last:
                dv = value_grad(made["mix", k][0], inv, p, before[1], after)
                gwos = [made["mix", c][2] for c in each]
                made["values"] = dv, value_project(order, dv, tokens, gwos)
                before, after = before[0:1], (made["values"][1][0],)
            made[name, k] = attend_back(
                chunks[k], made["mix", k][0], mix, inv, qa, ka, va, p, cosine, sine, before,
                k == last, after,
            )
            ready = made[name, k][0]

    for k in each:
        run("forward", k)
        if k:
            run("sum two", k - 1)
    if not last:
        run("sum two", 0)
    run("norm two", 0)
    if last:
        run("sum two", last)
        run("norm two", 1)
    run("back", 0)
    for k in each[1:]:
        if k > 1:
            run("norm two", k)
            run("sum one", k - 1)
        run("back", k)
        if k == 1:
            run("sum one", 0)
    run("weights", 0)
    if not last:
        run("sum one", 0)
    run("norm one", 0)
    if last:
        run("sum one", last)
    for k in each:
        run("mix", k)
        if k < last:
            run("norm one", k + 1)
        run("attend", k)

    dv, value_parts = made["values"]
    dqs, dk = [made["attend", k][0] for k in each], made["attend", last][1]
    picks = [made["mix", k][1] for k in each]
    near_outs = [made["norm two", k][0] for k in each]
    sums = add_sums(
        [made["norm one", k][2] for k in each], [made["norm two", k][2] for k in each],
        [made["back", k][3] for k in each],
    )
    key_parts = key_project(chunks, order, dqs, dk, dv, tokens, sums, swap(sums, "mp", 1))
    shares = me ^ jnp.array([0, 2, 1, 3], jnp.int32)
    here, there = input_grads(chunks, shares, dqs, dk, dv, wq, wk, wv, (key_parts[0],))
    send, keep = token_grads(chunks, here, swap(there, "mp", 1), picks)
    grad_tokens = keep + swap(send, "mp", 2).astype(f32)
    far_outs = [swap(x, "mp", 1) for x in near_outs]
    layer_out = place(chunks, where, near_outs, far_outs, n, (send,))

    if stepwise:
        grads = scatter_sum(*made["weights"])[0]
        grad_w_in, grad_w_down = grads[0], grads[1]
        value_parts = gather(scatter_sum(*value_parts).astype(bf16))
        key_parts = gather(scatter_sum(*key_parts).astype(bf16))
    else:
        grad_w_in, grad_w_down = (
            lax.psum_scatter(
                made["weights"][0][0, k].astype(f32), "dp", scatter_dimension=0, tiled=True
            )
            for k in range(2)
        )
        value_parts, key_parts = (
            [lax.psum(part.astype(f32), "dp").astype(bf16) for part in parts_of]
            for parts_of in (value_parts, key_parts)
        )
    gv, go = settle(order, value_parts, w)
    gq, gk, sums = settle(order, key_parts, w, sums=True)
    g1, s1, bo, g2, s2, bd, bi, qkv = (sums[k] for k in range(8))
    return (
        layer_out, grad_tokens.T, gq.T, qkv[0:w], gk.T, qkv[w : 2 * w], gv.T, qkv[2 * w : 3 * w],
        go, bo, g1, s1, grad_w_in, bi, grad_w_down.T, bd, g2, s2,
    )


def solution(mesh):
    in_specs = (
        P("dp", None), P("dp", None),
        P(None, "mp"), P("mp"), P(None, "mp"), P("mp"), P(None, "mp"), P("mp"),
        P("mp", None), P(), P(), P(),
        P("dp", "mp"), P("mp"), P("mp", "dp"), P(), P(), P(),
        P("dp", None),
    )
    out_specs = (
        P("dp", None), P("dp", "mp"),
        P(None, "mp"), P("mp"), P(None, "mp"), P("mp"), P(None, "mp"), P("mp"),
        P("mp", None), P(), P(), P(),
        P("dp", "mp"), P("mp"), P("mp", "dp"), P(), P(), P(),
    )
    return jax.shard_map(shards, mesh=mesh, in_specs=in_specs, out_specs=out_specs, check_vma=False)
```

```python
from functools import partial
import math

import jax
import jax.numpy as jnp
from jax import lax
from jax.experimental import pallas as pl
from jax.experimental.pallas import tpu as pltpu
from jax.sharding import PartitionSpec as P

HEAD_DIM = 64
HALF_DIM = HEAD_DIM // 2
WIDE = 128
USED = 80
MASKED = -1e30
LOG2E = math.log2(math.e)
EPS = 1e-12
BLOCK = 256
B_OUT, GAIN1, SHIFT1, B_IN, B_DOWN, GAIN2, SHIFT2 = (slice(k, k + 1) for k in range(7))
bf16 = jnp.bfloat16
f32 = jnp.float32
VMEM = pl.BlockSpec(memory_space=pltpu.VMEM)
SMEM = pl.BlockSpec(memory_space=pltpu.SMEM)
ANY = pl.BlockSpec(memory_space=pl.ANY)
HBM = pl.BlockSpec(memory_space=pltpu.HBM)
TURNS = (
    "values", "keys", "values", "weights", "keys", "values", "keys", "values", "keys", "keys"
)
SHARE = 1e9


def launch(body, args, in_specs, out_shape, out_specs, *, mib, us, after=(), scalars=0, grid=(), scratch=(), aliases=None):
    taken, waits = len(args), len(after)

    def run(*refs):
        body(*refs[:taken], *refs[taken + waits :])

    return pl.pallas_call(
        run,
        grid_spec=pltpu.PrefetchScalarGridSpec(
            num_scalar_prefetch=scalars,
            grid=grid,
            in_specs=list(in_specs) + [ANY] * waits,
            out_specs=out_specs,
            scratch_shapes=list(scratch),
        ),
        out_shape=out_shape,
        input_output_aliases=aliases or {},
        compiler_params=pltpu.CompilerParams(vmem_limit_bytes=mib * 2**20),
        cost_estimate=pl.CostEstimate(flops=int(us * SHARE), bytes_accessed=0, transcendentals=0),
    )(*args, *after)


def out(*shape, dtype=bf16):
    return jax.ShapeDtypeStruct(shape, dtype)


def dot(left, right, left_dim, right_dim):
    return lax.dot_general(
        left, right, (((left_dim,), (right_dim,)), ((), ())), preferred_element_type=f32
    )


def qkv_body(
    len_ref, tok_hbm, wq_hbm, wk_hbm, wv_hbm, bq_ref, bk_ref, bv_ref,
    qa_ref, ka_ref, va_ref, cos_ref, sin_ref, tok_ref, w_ref, sems,
):
    copies = [
        pltpu.make_async_copy(from_ref, to_ref, sems.at[k])
        for k, (from_ref, to_ref) in enumerate((
            (tok_hbm, tok_ref), (wq_hbm, w_ref.at[0]), (wk_hbm, w_ref.at[1]), (wv_hbm, w_ref.at[2])
        ))
    ]
    for copy in copies:
        copy.start()
    n = tok_ref.shape[0]
    heads = w_ref.shape[1] // HEAD_DIM
    pos = lax.broadcasted_iota(jnp.int32, (1, n), 1)
    first = len_ref[0, 0]
    used = first + len_ref[0, 1]
    in0, in1 = pos < first, pos < used
    start = jnp.where(in0, 0, jnp.where(in1, first, used))
    index = lax.broadcasted_iota(jnp.int32, (HALF_DIM, 1), 0).astype(f32)
    freq = jnp.exp(index * (-math.log(10000.0) / HALF_DIM))
    angles = freq * (pos - start).astype(f32)
    cosine, sine = jnp.cos(angles), jnp.sin(angles)
    cos_ref[...] = cosine
    sin_ref[...] = sine
    segment = jnp.where(in0, 0, jnp.where(in1, 1, 2))
    row = lax.broadcasted_iota(jnp.int32, (WIDE - HEAD_DIM, n), 0)
    same = row == segment
    q_tail = jnp.where(same, 1.0, 0.0).astype(bf16)
    k_tail = jnp.where(jnp.logical_or(same, row > 2), 0.0, MASKED).astype(bf16)
    v_tail = jnp.where(row < 3, 1.0, 0.0).astype(bf16)

    def rotated(lin, h, scale):
        a = lin[h * HEAD_DIM : h * HEAD_DIM + HALF_DIM]
        b = lin[h * HEAD_DIM + HALF_DIM : (h + 1) * HEAD_DIM]
        x, y = a * cosine - b * sine, b * cosine + a * sine
        if scale != 1.0:
            x, y = x * scale, y * scale
        return x.astype(bf16), y.astype(bf16)

    copies[0].wait()
    for k, (b_ref, to_ref, tail, scale) in enumerate((
        (bq_ref, qa_ref, q_tail, LOG2E / math.sqrt(HEAD_DIM)),
        (bk_ref, ka_ref, k_tail, 1.0),
        (bv_ref, va_ref, v_tail, None),
    )):
        copies[1 + k].wait()
        column = jnp.broadcast_to(b_ref[...].reshape(1, -1), (8, b_ref.shape[0])).T[:, 0:1]
        lin = dot(w_ref[k], tok_ref[...], 1, 1) + column
        for h in range(heads):
            if scale is None:
                to_ref[h, 0:HEAD_DIM] = lin[h * HEAD_DIM : (h + 1) * HEAD_DIM].astype(bf16)
            else:
                x, y = rotated(lin, h, scale)
                to_ref[h, 0:HALF_DIM] = x
                to_ref[h, HALF_DIM:HEAD_DIM] = y
            to_ref[h, HEAD_DIM:] = tail


def project(lengths, tok, wq, wk, wv, bq, bk, bv):
    n = tok.shape[0]
    heads = wq.shape[0] // HEAD_DIM
    return launch(
        qkv_body, (lengths, tok, wq, wk, wv, bq, bk, bv), [SMEM] + [HBM] * 4 + [VMEM] * 3,
        (
            out(heads, WIDE, n), out(heads, WIDE, n), out(heads, WIDE, n),
            out(HALF_DIM, n, dtype=f32), out(HALF_DIM, n, dtype=f32),
        ),
        (VMEM,) * 5, mib=63, us=5,
        scratch=[
            pltpu.VMEM(tok.shape, bf16), pltpu.VMEM((3, *wq.shape), bf16),
            pltpu.SemaphoreType.DMA((4,)),
        ],
    )


def chunk_block(chunk, half_blocks):
    first, count = chunk
    return lambda i: (i // count) * half_blocks + first + lax.rem(i, count)


def attend_body(qa_ref, ka_ref, va_ref, p_ref, mix_ref, inv_ref):
    heads, _, n = ka_ref.shape
    pieces = [slice(at, at + n // 3) for at in range(0, n, n // 3)]

    def score(h):
        scores = [dot(ka_ref[h, :, piece], qa_ref[h], 0, 0) for piece in pieces]
        top = jnp.max(scores[0], axis=0, keepdims=True)
        for s in scores[1:]:
            top = jnp.maximum(top, jnp.max(s, axis=0, keepdims=True))
        return scores, top

    def mix(h, scores, top):
        mixed = None
        for piece, s in zip(pieces, scores):
            p = jnp.exp2(s - top).astype(bf16)
            p_ref[h, piece] = p
            term = jnp.dot(va_ref[h, 0:USED, piece], p, preferred_element_type=f32)
            mixed = term if mixed is None else mixed + term
        inv = 1.0 / mixed[HEAD_DIM : HEAD_DIM + 1]
        mix_ref[h * HEAD_DIM : (h + 1) * HEAD_DIM] = (mixed[0:HEAD_DIM] * inv).astype(bf16)
        inv_ref[h] = inv

    following = score(0)
    for h in range(heads):
        current = following
        if h + 1 < heads:
            following = score(h + 1)
        mix(h, *current)


def attend(chunk, qa, ka, va, after=()):
    heads, _, n = qa.shape
    block = chunk_block(chunk, n // BLOCK // 2)
    steps = 2 * chunk[1]
    width = steps * BLOCK
    return launch(
        attend_body, (qa, ka, va),
        [pl.BlockSpec((heads, WIDE, BLOCK), lambda i: (0, 0, block(i))), VMEM, VMEM],
        (out(heads, n, width), out(heads * HEAD_DIM, width), out(heads, 1, width, dtype=f32)),
        (
            pl.BlockSpec((heads, n, BLOCK), lambda i: (0, 0, i)),
            pl.BlockSpec((heads * HEAD_DIM, BLOCK), lambda i: (0, i)),
            pl.BlockSpec((heads, 1, BLOCK), lambda i: (0, 0, i)),
        ),
        mib=56, us=2.4 * steps, grid=(steps,), after=after,
    )


def attend_back_body(
    last, do_ref, mix_ref, inv_ref, qa_ref, ka_ref, va_ref, p_ref, cos_ref, sin_ref, *refs
):
    if last:
        cos_all, sin_all, before, dq_ref, to_ref, dk_ref = refs
        held = ((dk_ref, before),)
    else:
        *before, dq_ref, dk_ref, dv_ref = refs
        held = tuple(zip((dk_ref, dv_ref), before or (None, None)))
    heads, _, width = qa_ref.shape
    n = ka_ref.shape[2]
    pieces = [slice(at, at + n // 3) for at in range(0, n, n // 3)]

    @pl.when(pl.program_id(0) == 0)
    def _():
        for acc, start in held:
            acc[...] = jnp.zeros_like(acc) if start is None else start[...]

    def score_grad(h):
        rows = slice(h * HEAD_DIM, (h + 1) * HEAD_DIM)
        do = (do_ref[rows].astype(f32) * inv_ref[h]).astype(bf16)
        delta = jnp.sum(do.astype(f32) * mix_ref[rows].astype(f32), axis=0, keepdims=True)
        d1 = delta.astype(bf16).astype(f32)
        d2 = (delta - d1).astype(bf16).astype(f32)
        d3 = delta - d1 - d2
        row = lax.broadcasted_iota(jnp.int32, (USED - HEAD_DIM, width), 0)
        tail = jnp.where(row == 0, -d1, jnp.where(row == 1, -d2, jnp.where(row == 2, -d3, 0.0)))
        do_wide = jnp.concatenate([do, tail.astype(bf16)], axis=0)
        return do, [dot(va_ref[h, 0:USED, piece], do_wide, 0, 0) for piece in pieces]

    def finish(h, do, grads):
        lo, mid, hi = h * HEAD_DIM, h * HEAD_DIM + HALF_DIM, (h + 1) * HEAD_DIM
        dq = None
        for piece, dp in zip(pieces, grads):
            p = p_ref[h, piece]
            ds = (p.astype(f32) * dp).astype(bf16)
            term = jnp.dot(ka_ref[h, 0:HEAD_DIM, piece], ds, preferred_element_type=f32)
            dq = term if dq is None else dq + term
            dk_ref[lo:hi, piece] += dot(qa_ref[h, 0:HEAD_DIM], ds, 1, 1)
            if not last:
                dv_ref[lo:hi, piece] += dot(do, p, 1, 1)
        dq = dq * (1.0 / math.sqrt(HEAD_DIM))
        dq_ref[lo:mid], dq_ref[mid:hi] = turned_back(
            dq[0:HALF_DIM], dq[HALF_DIM:HEAD_DIM], cos_ref[...], sin_ref[...]
        )

    following = score_grad(0)
    for h in range(heads):
        current = following
        if h + 1 < heads:
            following = score_grad(h + 1)
        finish(h, *current)
    if last:

        @pl.when(pl.program_id(0) == pl.num_programs(0) - 1)
        def _():
            for lo in range(0, dk_ref.shape[0], HEAD_DIM):
                mid, hi = lo + HALF_DIM, lo + HEAD_DIM
                a, b = dk_ref[lo:mid] * math.log(2.0), dk_ref[mid:hi] * math.log(2.0)
                to_ref[lo:mid], to_ref[mid:hi] = turned_back(a, b, cos_all[...], sin_all[...])


def turned_back(a, b, cosine, sine):
    return (a * cosine + b * sine).astype(bf16), (b * cosine - a * sine).astype(bf16)


def attend_back(chunk, do, mix, inv, qa, ka, va, p, cosine, sine, before, last, after=()):
    heads, _, n = qa.shape
    w = heads * HEAD_DIM
    block = chunk_block(chunk, n // BLOCK // 2)
    steps = 2 * chunk[1]
    columns = pl.BlockSpec((w, BLOCK), lambda i: (0, i))
    table = pl.BlockSpec((HALF_DIM, BLOCK), lambda i: (0, block(i)))
    before = (cosine, sine, *before) if last else before
    shapes = (out(w, steps * BLOCK), out(w, n)) if last else (
        out(w, steps * BLOCK), out(w, n, dtype=f32), out(w, n, dtype=f32)
    )
    return launch(
        partial(attend_back_body, last),
        (do, mix, inv, qa, ka, va, p, cosine, sine, *before),
        [
            columns,
            columns,
            pl.BlockSpec((heads, 1, BLOCK), lambda i: (0, 0, i)),
            pl.BlockSpec((heads, WIDE, BLOCK), lambda i: (0, 0, block(i))),
            VMEM,
            VMEM,
            pl.BlockSpec((heads, n, BLOCK), lambda i: (0, 0, i)),
            table,
            table,
        ] + [VMEM] * len(before),
        shapes, (columns,) + (VMEM,) * (len(shapes) - 1),
        mib=32, us=3 * steps, grid=(steps,), after=after,
        scratch=[pltpu.VMEM((w, n), f32)] if last else (),
    )


def value_grad_body(do_ref, inv_ref, p_ref, before, to_ref, acc):
    step = pl.program_id(0)

    @pl.when(step == 0)
    def _():
        acc[...] = before[...]

    for h in range(p_ref.shape[0]):
        rows = slice(h * HEAD_DIM, (h + 1) * HEAD_DIM)
        do = (do_ref[rows].astype(f32) * inv_ref[h]).astype(bf16)
        acc[rows] += dot(do, p_ref[h], 1, 1)

    @pl.when(step == pl.num_programs(0) - 1)
    def _():
        to_ref[...] = acc[...].astype(bf16)


def value_grad(do, inv, p, before, after=()):
    heads, n, width = p.shape
    w = heads * HEAD_DIM
    return launch(
        value_grad_body, (do, inv, p, before),
        [
            pl.BlockSpec((w, BLOCK), lambda i: (0, i)),
            pl.BlockSpec((heads, 1, BLOCK), lambda i: (0, 0, i)),
            pl.BlockSpec((heads, n, BLOCK), lambda i: (0, 0, i)),
            VMEM,
        ],
        out(w, n), VMEM, mib=20, us=2, grid=(width // BLOCK,), after=after,
        scratch=[pltpu.VMEM((w, n), f32)],
    )


def by_run(chunk, other):
    return lambda i, where: lax.rem(where[0] + other, 2) * chunk[1] + i


def assemble(order, pieces, which, after=()):
    rows, d = pieces[0].shape[2:]
    count, parts = len(pieces), sum(piece.shape[0] for piece in pieces)

    def body(order_ref, *refs):
        to_ref = refs[count]
        held = [(ref, k) for ref in refs[0:count] for k in range(ref.shape[0])]
        for j, (ref, k) in enumerate(held):
            to_ref[pl.ds(pl.multiple_of(order_ref[j] * rows, rows), rows)] = ref[k, which]

    return launch(
        body, (order, *pieces), [SMEM] + [VMEM] * count, out(parts * rows, d), VMEM,
        mib=12, us=0.6, after=after,
    )


def hold(arrays, after=()):
    count = len(arrays)

    def body(*refs):
        for from_ref, to_ref in zip(refs[:count], refs[count:]):
            to_ref[...] = from_ref[...]

    return launch(
        body, arrays, [VMEM] * count, tuple(out(*x.shape) for x in arrays), (VMEM,) * count,
        mib=8, us=0.5, after=after,
    )


def add_body(a_ref, b_ref, to_ref):
    to_ref[...] = (a_ref[...].astype(f32) + b_ref[...].astype(f32)).astype(bf16)


def add_low(a, b, after=()):
    return launch(
        add_body, (a, b), [VMEM] * 2, out(*a.shape), VMEM, mib=8, us=0.5, after=after
    )


def add_parts(keep, came, last, after=()):
    parts, *shape = keep.shape

    def body(keep_ref, came_ref, *to_refs):
        result = keep_ref[...].astype(f32) + came_ref[...].astype(f32)
        if last:
            to_refs[0][...] = result
        else:
            to_refs[0][...] = result[0 : parts // 2].astype(bf16)
            to_refs[1][...] = result[parts // 2 :].astype(bf16)

    shapes = (out(*keep.shape, dtype=f32),) if last else (out(parts // 2, *shape),) * 2
    return launch(
        body, (keep, came), [VMEM] * 2, shapes, (VMEM,) * len(shapes), mib=12, us=0.8, after=after
    )


def add_wide(a, b, after=()):
    def body(a_ref, b_ref, to_ref):
        to_ref[...] = a_ref[...] + b_ref[...].astype(f32)

    return launch(
        body, (a, b), [VMEM] * 2, out(*a.shape, dtype=f32), VMEM, mib=8, us=0.8, after=after
    )


def stack_rows(vectors, after=()):
    def body(*refs):
        *from_refs, to_ref = refs
        to_ref[...] = jnp.zeros_like(to_ref)
        for k, ref in enumerate(from_refs):
            to_ref[k : k + 1] = ref[...].reshape(1, -1)

    return launch(
        body, tuple(vectors), [VMEM] * len(vectors), out(8, vectors[0].shape[0], dtype=f32), VMEM,
        mib=4, us=1, after=after,
    )


def join_body(a_ref, b_ref, to_ref):
    k = a_ref.shape[0]
    to_ref[0:k] = a_ref[...]
    to_ref[k:] = b_ref[...]


def join(a, b, after=()):
    return launch(
        join_body, (a, b), [VMEM, VMEM], out(a.shape[0] + b.shape[0], *a.shape[1:]), VMEM,
        mib=8, us=0.5, after=after,
    )


def forward_body(*refs):
    where_ref, *refs = refs
    mixes, outs = refs[0:8], refs[8:12]
    (tok_ref, vec_ref, wi_ref, wd_ref,
     low_ref, unit_ref, scale_ref, act_ref, slope_ref, own_ref, other_ref) = refs[12:]

    def norm(k):
        z = tok_ref[k].astype(f32) + vec_ref[B_OUT]
        for mix_ref, wo_ref in zip(mixes[k::2], outs):
            z = z + dot(mix_ref[...], wo_ref[...], 0, 0)
        center = z - jnp.mean(z, axis=-1, keepdims=True)
        scale = lax.rsqrt(jnp.mean(center * center, axis=-1, keepdims=True) + EPS)
        unit = center * scale
        low = (unit * vec_ref[GAIN1] + vec_ref[SHIFT1]).astype(bf16)
        low_ref[k] = low
        if k == 0:
            unit_ref[...] = unit.astype(bf16)
            scale_ref[...] = scale
        return low

    def expand(k, low):
        return jnp.dot(low, wi_ref[...], preferred_element_type=f32) + vec_ref[B_IN]

    def activate(k, inner):
        phi = 0.5 * lax.erf(inner * math.sqrt(0.5)) + 0.5
        bell = jnp.exp2(inner * inner * (-0.5 * LOG2E)) * (1.0 / math.sqrt(2.0 * math.pi))
        act = (inner * phi).astype(bf16)
        act_ref[k] = act
        slope_ref[k] = (phi + inner * bell).astype(bf16)
        return act

    def contract(k, act):
        (own_ref, other_ref)[k][...] = dot(act, wd_ref[...], 1, 1).astype(bf16)

    low_b = norm(1)
    inner_b = expand(1, low_b)
    low_a = norm(0)
    act_b = activate(1, inner_b)
    inner_a = expand(0, low_a)
    contract(1, act_b)
    contract(0, activate(0, inner_a))


def split_tokens(chunks, where, tok, after=()):
    n, d = tok.shape
    runs = slot_runs(chunks, n)

    def body(where_ref, tok_ref, *to_refs):
        for to_ref, (first, _, length) in zip(to_refs, runs):
            for k in range(2):
                half = where_ref[0] if k == 0 else 1 - where_ref[0]
                at = pl.multiple_of(half * (n // 2) + first, BLOCK)
                to_ref[k] = tok_ref[pl.ds(at, length)]

    return launch(
        body, (where, tok), [SMEM, VMEM], tuple(out(2, length, d) for _, _, length in runs),
        (VMEM,) * len(runs), mib=12, us=1, after=after,
    )


def feed_forward(chunk, where, mixes, outs, tok, vec, wi, wd, after=()):
    _, _, d = tok.shape
    hidden = wi.shape[1]
    count = chunk[1]
    rows = count * BLOCK
    w = mixes[0].shape[0]
    own_run, other_run = by_run(chunk, 0), by_run(chunk, 1)
    mix_specs, mix_args = [], []
    for m in mixes:
        mix_specs += [
            pl.BlockSpec((w, BLOCK), lambda i, where: (0, own_run(i, where))),
            pl.BlockSpec((w, BLOCK), lambda i, where: (0, other_run(i, where))),
        ]
        mix_args += [m, m]
    both = lambda width: pl.BlockSpec((2, BLOCK, width), lambda i, where: (0, i, 0))
    one = lambda width: pl.BlockSpec((BLOCK, width), lambda i, where: (i, 0))
    return launch(
        forward_body, (where, *mix_args, *outs, tok, vec, wi, wd),
        mix_specs + [VMEM] * 4 + [
            pl.BlockSpec((2, BLOCK, d), lambda i, where: (0, i, 0)),
        ] + [VMEM] * 3,
        (
            out(2, rows, d), out(rows, d), out(rows, 1, dtype=f32), out(2, rows, hidden),
            out(2, rows, hidden), out(rows, d), out(rows, d),
        ),
        (both(d), one(d), one(1), both(hidden), both(hidden), one(d), one(d)),
        mib=24, us=4.5 * count, scalars=1, grid=(count,), after=after,
    )


def norm_back(g, unit, scale, gain):
    q = g * gain
    return scale * (
        q - jnp.mean(q, axis=-1, keepdims=True) - unit * jnp.mean(q * unit, axis=-1, keepdims=True)
    )


def put_sums(sums_ref, *terms):
    sums_ref[...] = jnp.zeros_like(sums_ref)
    for k, term in enumerate(terms):
        sums_ref[k : k + 1] = jnp.sum(term, axis=0, keepdims=True)


def second_norm_body(
    first, where_ref, len_ref, unit_ref, mine_ref, theirs_ref, vec_ref, cot_ref,
    out_ref, low_ref, sums_ref, held, sem,
):
    rows = unit_ref.shape[0]
    half = cot_ref.shape[0] // 2
    start = pl.multiple_of(where_ref[0] * half + first, BLOCK)
    copy = pltpu.make_async_copy(cot_ref.at[pl.ds(start, rows)], held, sem)
    copy.start()
    total = mine_ref[...].astype(f32) + theirs_ref[...].astype(f32)
    z = unit_ref[...].astype(f32) * vec_ref[GAIN1] + vec_ref[SHIFT1] + total + vec_ref[B_DOWN]
    center = z - jnp.mean(z, axis=-1, keepdims=True)
    scale = lax.rsqrt(jnp.mean(center * center, axis=-1, keepdims=True) + EPS)
    unit = center * scale
    out_ref[...] = (unit * vec_ref[GAIN2] + vec_ref[SHIFT2]).astype(bf16)
    slot = start + lax.broadcasted_iota(jnp.int32, (rows, 1), 0)
    copy.wait()
    g = jnp.where(slot < len_ref[0, 0] + len_ref[0, 1], held[...], 0.0)
    back = norm_back(g, unit, scale, vec_ref[GAIN2])
    low_ref[...] = back.astype(bf16)
    put_sums(sums_ref, g * unit, g, back)


def second_norm(chunk, where, lengths, unit, mine, theirs, vec, cot, after=()):
    rows, d = unit.shape
    return launch(
        partial(second_norm_body, chunk[0] * BLOCK),
        (where, lengths, unit, mine, theirs, vec, cot), [SMEM] * 2 + [VMEM] * 4 + [HBM],
        (out(rows, d), out(rows, d), out(8, d, dtype=f32)), (VMEM,) * 3,
        mib=12, us=2, after=after,
        scratch=[pltpu.VMEM((rows, d), f32), pltpu.SemaphoreType.DMA(())],
    )


def first_norm_body(unit_ref, scale_ref, vec_ref, skip_ref, mine_ref, theirs_ref, low_ref, sums_ref):
    g = skip_ref[...].astype(f32) + (mine_ref[...].astype(f32) + theirs_ref[...].astype(f32))
    unit = unit_ref[...].astype(f32)
    back = norm_back(g, unit, scale_ref[...], vec_ref[GAIN1])
    low_ref[...] = back.astype(bf16)
    put_sums(sums_ref, g * unit, g, back)


def first_norm(unit, scale, vec, skip, mine, theirs, after=()):
    rows, d = skip.shape
    return launch(
        first_norm_body, (unit, scale, vec, skip, mine, theirs), [VMEM] * 6,
        (out(rows, d), out(8, d, dtype=f32)), (VMEM,) * 2, mib=12, us=1, after=after,
    )


def backward_body(near_ref, far_ref, wi_ref, wd_ref, slope_ref, gi_ref, own_ref, other_ref, sums_ref):
    def open_up(k):
        return jnp.dot((near_ref, far_ref)[k][...], wd_ref[...], preferred_element_type=f32)

    def slopes(k, g):
        g = (g * slope_ref[k].astype(f32)).astype(bf16)
        gi_ref[k] = g
        return g

    def close(k, g):
        (own_ref, other_ref)[k][...] = dot(g, wi_ref[...], 1, 1).astype(bf16)

    open_b = open_up(1)
    open_a = open_up(0)
    g_b = slopes(1, open_b)
    close(1, g_b)
    g_a = slopes(0, open_a)
    close(0, g_a)
    put_sums(sums_ref, g_a.astype(f32) + g_b.astype(f32))


def feed_back(near_low, far_low, wi, wd, slope, after=()):
    rows, d = near_low.shape
    hidden = slope.shape[2]
    return launch(
        backward_body, (near_low, far_low, wi, wd, slope), [VMEM] * 5,
        (out(2, rows, hidden), out(rows, d), out(rows, d), out(8, hidden, dtype=f32)),
        (VMEM,) * 4, mib=12, us=1.6, after=after,
    )


def weight_grad_body(order_ref, *refs):
    chunks = (len(refs) - 2) // 5 if len(refs) % 5 == 2 else (len(refs) - 3) // 5
    lows, gis, acts = refs[0:chunks], refs[chunks : 2 * chunks], refs[2 * chunks : 3 * chunks]
    nears, fars = refs[3 * chunks : 4 * chunks], refs[4 * chunks : 5 * chunks]
    *to_refs, grad_ref = refs[5 * chunks :]

    def spread(which):
        first = to_refs[0].shape[0]
        rows = to_refs[0].shape[2]
        for j in range(order_ref.shape[0]):
            to_ref, k = (to_refs[0], j) if j < first else (to_refs[1], j - first)
            at = pl.ds(pl.multiple_of(order_ref[j] * rows, rows), rows)
            to_ref[k, which] = grad_ref[at].astype(bf16)

    total = None
    for low_ref, gi_ref in zip(lows, gis):
        for k in range(2):
            term = dot(low_ref[k], gi_ref[k], 0, 0)
            total = term if total is None else total + term
    grad_ref[...] = total
    spread(0)
    total = None
    for near_ref, far_ref, act_ref in zip(nears, fars, acts):
        term = dot(near_ref[...], act_ref[0], 0, 0) + dot(far_ref[...], act_ref[1], 0, 0)
        total = term if total is None else total + term
    grad_ref[...] = total
    spread(1)


def weight_grads(order, lows, gis, acts, nears, fars, after=()):
    d, hidden = lows[0].shape[2], gis[0].shape[2]
    width = BLOCK
    parts = order.shape[0]
    sizes = (1,) if parts == 1 else (parts // 2, parts // 2)
    rows = d // parts
    wide = [pl.BlockSpec((2, a.shape[1], width), lambda i, order: (0, 0, i)) for a in gis]
    return launch(
        weight_grad_body, (order, *lows, *gis, *acts, *nears, *fars),
        [VMEM] * len(lows) + wide + wide + [VMEM] * (2 * len(lows)),
        tuple(out(k, 2, rows, hidden) for k in sizes),
        tuple(pl.BlockSpec((k, 2, rows, width), lambda i, order: (0, 0, 0, i)) for k in sizes),
        mib=20, us=6, scalars=1, grid=(hidden // width,),
        scratch=[pltpu.VMEM((d, width), f32)], after=after,
    )


def mix_back_body(where_ref, near_ref, far_ref, wo_ref, mix_ref, do_ref, pick_ref, gwo_ref):
    w, d = wo_ref.shape

    @pl.when(pl.program_id(0) == 0)
    def _():
        gwo_ref[...] = jnp.zeros_like(gwo_ref)

    row = lax.broadcasted_iota(jnp.int32, (w, d), 0) + where_ref[1] * w
    chosen = jnp.where(row == lax.broadcasted_iota(jnp.int32, (w, d), 1), 1.0, 0.0).astype(bf16)

    def run(from_ref):
        g = from_ref[...]
        do_ref[...] = dot(wo_ref[...], g, 1, 1).astype(bf16)
        pick_ref[...] = dot(chosen, g, 1, 1).astype(bf16)
        gwo_ref[...] += jnp.dot(mix_ref[...], g, preferred_element_type=f32)

    @pl.when(pl.program_id(0) == where_ref[0])
    def _():
        run(near_ref)

    @pl.when(pl.program_id(0) != where_ref[0])
    def _():
        run(far_ref)


def mix_back(where, near_half, far_half, wo, mix, after=()):
    rows, d = near_half.shape
    w = wo.shape[0]
    columns = pl.BlockSpec((w, rows), lambda i, where: (0, i))
    return launch(
        mix_back_body, (where, near_half, far_half, wo, mix), [VMEM, VMEM, VMEM, columns],
        (out(w, 2 * rows), out(w, 2 * rows), out(w, d, dtype=f32)),
        (columns, columns, pl.BlockSpec((w, d), lambda i, where: (0, 0))),
        mib=12, us=2, scalars=1, grid=(2,), after=after,
    )


def slot_runs(chunks, n):
    return [(first * BLOCK, n // 2 + first * BLOCK, count * BLOCK) for first, count in chunks]


def spread(order_ref, grad_ref, to_refs, rows):
    first = to_refs[0].shape[0]
    for j in range(order_ref.shape[0]):
        to_ref, k = (to_refs[0], j) if j < first else (to_refs[1], j - first)
        at = pl.ds(pl.multiple_of(order_ref[j] * rows, rows), rows)
        to_ref[k, 0:rows] = grad_ref[at].astype(bf16)


def total(refs):
    result = refs[0][...]
    for ref in refs[1:]:
        result = result + ref[...]
    return result


def split_parts(order):
    parts = order.shape[0]
    return (1,) if parts == 1 else (parts // 2, parts // 2)


def value_project(order, dv, tok, gwos, after=()):
    w, d = gwos[0].shape
    sizes = split_parts(order)
    count = len(gwos)

    def body(order_ref, dv_ref, tok_ref, *refs):
        *to_refs, grad_ref = refs[count:]
        grad_ref[0:w] = jnp.dot(dv_ref[...], tok_ref[...], preferred_element_type=f32)
        grad_ref[w:] = total(refs[0:count])
        spread(order_ref, grad_ref, to_refs, 2 * w // order_ref.shape[0])

    return launch(
        body, (order, dv, tok, *gwos), [SMEM] + [VMEM] * (2 + count),
        tuple(out(k, 2 * w // sum(sizes), d) for k in sizes), (VMEM,) * len(sizes),
        mib=16, us=1.5, scratch=[pltpu.VMEM((2 * w, d), f32)], after=after,
    )


def key_project(chunks, order, dqs, dk, dv, tok, sums, far_sums, after=()):
    w, n = dk.shape
    d = tok.shape[1]
    sizes = split_parts(order)
    count = len(dqs)
    parts = sum(sizes)
    rows = 2 * w // parts
    runs = slot_runs(chunks, n)

    def body(order_ref, dk_ref, dv_ref, tok_ref, sums_ref, far_ref, *refs):
        dq_refs, (*to_refs, grad_ref, vec_ref) = refs[0:count], refs[count:]
        ones = jnp.ones((8, n), bf16)
        grad = row = None
        for dq_ref, (first, second, length) in zip(dq_refs, runs):
            bias = dot(ones[:, 0 : 2 * length], dq_ref[...], 1, 1)
            row = bias if row is None else row + bias
            for k, at in enumerate((first, second)):
                term = jnp.dot(
                    dq_ref[:, k * length : (k + 1) * length], tok_ref[at : at + length],
                    preferred_element_type=f32,
                )
                grad = term if grad is None else grad + term
        grad_ref[0:w] = grad
        grad_ref[w:] = jnp.dot(dk_ref[...], tok_ref[...], preferred_element_type=f32)
        vec_ref[...] = sums_ref[...]
        vec_ref[0:6] = sums_ref[0:6] + far_ref[0:6]
        biases = [row, dot(ones, dk_ref[...], 1, 1), dot(ones, dv_ref[...], 1, 1)]
        biases.append(jnp.zeros((8, d - 3 * w), f32))
        vec_ref[7:8] = jnp.concatenate(biases, axis=1)[0:1]
        spread(order_ref, grad_ref, to_refs, rows)
        for j in range(parts):
            to_ref, k = (to_refs[0], j) if j < sizes[0] else (to_refs[1], j - sizes[0])
            tail = vec_ref[...] if parts == 1 else jnp.broadcast_to(
                vec_ref[pl.ds(order_ref[j], 1)], (8, d)
            )
            to_ref[k, rows:] = jnp.concatenate([tail, tail], axis=0).astype(bf16)

    return launch(
        body, (order, dk, dv, tok, sums, far_sums, *dqs), [SMEM] + [VMEM] * (5 + count),
        tuple(out(k, rows + 16, d) for k in sizes), (VMEM,) * len(sizes),
        mib=16, us=2, after=after,
        scratch=[pltpu.VMEM((2 * w, d), f32), pltpu.VMEM((8, d), f32)],
    )


def add_sums(ones, twos, ins, after=()):
    count = len(ones)

    def body(*refs):
        to_ref = refs[-1]
        to_ref[...] = jnp.zeros_like(to_ref)
        to_ref[0:3] = total([ref for ref in refs[0:count]])[0:3]
        to_ref[3:6] = total([ref for ref in refs[count : 2 * count]])[0:3]
        to_ref[6:7] = total([ref for ref in refs[2 * count : 3 * count]])[0:1]

    return launch(
        body, (*ones, *twos, *ins), [VMEM] * (3 * count), out(*ones[0].shape, dtype=f32), VMEM,
        mib=4, us=0.5, after=after,
    )


def input_grad_body(runs, share_ref, dk_ref, dv_ref, wq_ref, wk_ref, wv_ref, *refs):
    *dqs, here_ref, there_ref, all_ref = refs
    w = dk_ref.shape[0]
    for dq_ref, (first, second, length) in zip(dqs, runs):
        for k, at in enumerate((first, second)):
            slots = slice(at, at + length)
            part = dot(wq_ref[...], dq_ref[:, k * length : (k + 1) * length], 0, 0)
            part = part + dot(wk_ref[...], dk_ref[:, slots], 0, 0)
            all_ref[:, slots] = part + dot(wv_ref[...], dv_ref[:, slots], 0, 0)
    for j in range(4):
        at = pl.ds(pl.multiple_of(share_ref[j] * w, w), w)
        to_ref = here_ref if j < 2 else there_ref
        to_ref[j % 2] = all_ref[at].astype(bf16)


def input_grads(chunks, shares, dqs, dk, dv, wq, wk, wv, after=()):
    w, d = wq.shape
    n = dk.shape[1]
    return launch(
        partial(input_grad_body, slot_runs(chunks, n)), (shares, dk, dv, wq, wk, wv, *dqs),
        [SMEM] + [VMEM] * (5 + len(chunks)), (out(2, w, n), out(2, w, n)), (VMEM, VMEM),
        mib=20, us=3, scratch=[pltpu.VMEM((d, n), f32)], after=after,
    )


def token_grad_body(runs, here_ref, there_ref, *refs):
    *picks, send_ref, keep_ref = refs
    send_ref[...] = (here_ref[1].astype(f32) + there_ref[1].astype(f32)).astype(bf16)
    for pick_ref, (first, second, length) in zip(picks, runs):
        for k, at in enumerate((first, second)):
            slots = slice(at, at + length)
            keep_ref[:, slots] = (
                here_ref[0, :, slots].astype(f32) + there_ref[0, :, slots].astype(f32)
                + pick_ref[:, k * length : (k + 1) * length].astype(f32)
            )


def token_grads(chunks, here, there, picks, after=()):
    _, w, n = here.shape
    return launch(
        partial(token_grad_body, slot_runs(chunks, n)), (here, there, *picks),
        [VMEM] * (2 + len(chunks)), (out(w, n), out(w, n, dtype=f32)), (VMEM, VMEM),
        mib=12, us=1.5, after=after,
    )


def settle(order, pieces, w, sums=False, after=()):
    d = pieces[0].shape[-1]
    count, parts = len(pieces), order.shape[0]
    rows = 2 * w // parts

    def body(order_ref, *refs):
        from_refs, to_refs, all_ref, vec_ref = refs[0:count], refs[count:-2], refs[-2], refs[-1]
        held = [(ref, k) for ref in from_refs for k in range(ref.shape[0])]
        for j, (ref, k) in enumerate(held):
            at = pl.ds(pl.multiple_of(order_ref[j] * rows, rows), rows)
            all_ref[at] = ref[k, 0:rows].astype(f32)
            if sums:
                tail = ref[k, rows:].astype(f32)
                if parts == 1:
                    vec_ref[...] = tail[0:8]
                else:
                    vec_ref[pl.ds(order_ref[j], 1)] = tail[0:1]
        to_refs[0][...] = all_ref[0:w]
        to_refs[1][...] = all_ref[w:]
        if sums:
            for k in range(7):
                to_refs[2 + k][...] = vec_ref[k : k + 1].reshape(d)
            for k in range(3):
                to_refs[9 + k][...] = vec_ref[7:8, k * w : (k + 1) * w].reshape(w)

    shapes = (out(w, d, dtype=f32),) * 2
    if sums:
        shapes += (out(d, dtype=f32),) * 7 + (out(w, dtype=f32),) * 3
    return launch(
        body, (order, *pieces), [SMEM] + [VMEM] * count, shapes, (VMEM,) * len(shapes),
        mib=12, us=1, after=after,
        scratch=[pltpu.VMEM((2 * w, d), f32), pltpu.VMEM((8, d), f32)],
    )


def place_body(runs, where_ref, *refs):
    count = len(runs)
    nears, fars, to_ref = refs[0:count], refs[count : 2 * count], refs[-1]
    core = where_ref[0]
    half = to_ref.shape[0] // 2
    for near_ref, far_ref, (first, _, length) in zip(nears, fars, runs):
        for ref, owner in ((near_ref, core), (far_ref, 1 - core)):
            at = pl.ds(pl.multiple_of(owner * half + first, BLOCK), length)
            to_ref[at] = ref[...]


def place(chunks, where, nears, fars, n, after=()):
    d = nears[0].shape[1]
    return launch(
        partial(place_body, slot_runs(chunks, n)), (where, *nears, *fars),
        [SMEM] + [VMEM] * (2 * len(chunks)), out(n, d), VMEM, mib=12, us=2, after=after,
    )


def swap(x, axis, bit):
    return lax.ppermute(x, axis, [(i, i ^ bit) for i in range(lax.axis_size(axis))])


def split_slots(n):
    half_blocks = n // BLOCK // 2
    first = 0
    return [(0, first), (first, half_blocks - first)] if first else [(k, 1) for k in range(half_blocks)]


def shards(
    tokens, lengths, w_query, b_query, w_key, b_key, w_value, b_value, w_out, b_out, ln1_gain,
    ln1_bias, w_in, b_in, w_down, b_down, ln2_gain, ln2_bias, cotangent,
):
    dp = lax.axis_size("dp")
    n, d = tokens.shape
    w = w_query.shape[1]
    chunks = split_slots(n)
    me = lax.axis_index("mp")
    core = me % 2
    where = jnp.stack([core, me]).astype(jnp.int32)
    wq, wk, wv = w_query.T, w_key.T, w_value.T

    stepwise = dp & (dp - 1) == 0 and dp > 1 and (d // dp) % 16 == 0
    bits = [1 << k for k in range(dp.bit_length() - 1)] if stepwise else []
    parts = 1 << len(bits)
    order = jnp.zeros((1,), jnp.int32)
    if stepwise:
        count = len(bits)
        places = [
            sum(bit for k, bit in enumerate(bits) if j >> (count - 1 - k) & 1) for j in range(parts)
        ]
        order = lax.axis_index("dp") ^ jnp.array(places, jnp.int32)

    def sum_step(k, keep, send, *after):
        return add_parts(keep, swap(send, "dp", bits[k]), k + 1 == len(bits), after)

    vec = stack_rows([b_out, ln1_gain, ln1_bias, b_in, b_down, ln2_gain, ln2_bias])
    qa, ka, va, cosine, sine = project(lengths, tokens, wq, wk, wv, b_query, b_key, b_value)
    out_y = swap(w_out, "mp", 2)
    outs = (w_out, out_y, swap(w_out, "mp", 1), swap(out_y, "mp", 1))

    each, last = range(len(chunks)), len(chunks) - 1
    kept, mixes = [], []

    def run_attend(k, *after):
        kept.append(attend(chunks[k], qa, ka, va, after))
        mix = kept[k][1]
        mix_y = swap(mix, "mp", 2)
        mixes.append((mix, mix_y, swap(mix, "mp", 1), swap(mix_y, "mp", 1)))
        return kept[k][2]

    both = jnp.stack([w_in, w_down.T])[None]
    if stepwise:
        near, far, held = [both], [swap(both, "dp", bits[0])], both
        step = list(reversed(bits[1:]))

        def fetch(k, *after):
            nonlocal held, ready
            came = swap(held, "dp", step[k])
            if k + 1 < len(step):
                held = ready = join(held, came, (*after, far[-1]))
            else:
                (came,) = hold((came,), (*after, far[-1]))
                ready = came
            near.append(came)
            far.append(swap(came, "dp", bits[0]))

        ready = cosine
        for k in each:
            ready = run_attend(k, ready)
            if k < len(step):
                fetch(k, ready)
        for k in range(len(near) - 1, len(step)):
            fetch(k, ready)
        gathered = near + far
    else:
        ready = cosine
        for k in each:
            ready = run_attend(k, ready)
        gathered = [jnp.stack([
            lax.all_gather(part, "dp", axis=0, tiled=True) for part in (w_in, w_down.T)
        ])[None]]
    token_runs = split_tokens(chunks, where, tokens, (ready,))
    out_near, out_y = hold((w_out, out_y), (ready,))
    outs = (out_near, out_y, *outs[2:])
    came = [mix[1] for mix in mixes] + [token_runs[0], out_near]
    wi, wd = (assemble(order, gathered, k, (ready, *came)) for k in range(2))

    made = {}

    def run(name, k, *waits):
        nonlocal ready
        after = (ready, *waits)
        if name == "forward":
            made[name, k] = feed_forward(
                chunks[k], where, mixes[k], outs, token_runs[k], vec, wi, wd, after
            )
            ready = made[name, k][2]
        elif name == "sum two":
            *_, own, other = made["forward", k]
            mine = ready = add_low(own, swap(other, "mp", 1), after)
            made[name, k] = mine, swap(mine, "mp", 2)
        elif name == "norm two":
            made[name, k] = second_norm(
                chunks[k], where, lengths, made["forward", k][1], *made["sum two", k], vec,
                cotangent, after,
            )
            made["low", k] = made[name, k][1], swap(made[name, k][1], "mp", 1)
            ready = made[name, k][2]
        elif name == "back":
            made[name, k] = feed_back(*made["low", k], wi, wd, made["forward", k][4], after)
            ready = made[name, k][3]
        elif name == "sum one":
            _, own, other, _ = made["back", k]
            mine = ready = add_low(own, swap(other, "mp", 1), after)
            made[name, k] = mine, swap(mine, "mp", 2)
        elif name == "weights":
            forwards = [made["forward", c] for c in range(len(chunks))]
            nears, fars = zip(*(made["low", c] for c in range(len(chunks))))
            made[name] = weight_grads(
                order, [f[0] for f in forwards], [made["back", c][0] for c in range(len(chunks))],
                [f[3] for f in forwards], nears, fars, after,
            )
            ready = made[name][0]
        elif name == "norm one":
            forward = made["forward", k]
            half, sums = first_norm(
                forward[1], forward[2], vec, made["low", k][0], *made["sum one", k], after
            )
            made[name, k] = half, swap(half, "mp", 1), sums
            ready = sums
        elif name == "mix":
            made[name, k] = mix_back(where, *made["norm one", k][0:2], out_near, kept[k][1], after)
            ready = made[name, k][0]
        elif name == "values":
            gwos = [made["mix", c][2] for c in each]
            dv = value_grad(
                made["mix", last][0], kept[last][2], kept[last][0], made["attend", last - 1][2], after
            )
            made[name] = dv, value_project(order, dv, tokens, gwos)
            ready = made[name][1][0]
        elif name == "attend":
            p, mix, inv = kept[k]
            before = made[name, k - 1][1 : 2 if k == last else 3] if k else ()
            made[name, k] = attend_back(
                chunks[k], made["mix", k][0], mix, inv, qa, ka, va, p, cosine, sine, before,
                k == last, after,
            )
            ready = made[name, k][0]
        elif name == "weight sums":
            if stepwise and k < len(bits) - 1:
                made["weights"] = sum_step(k, *made["weights"], *after)
                ready = made["weights"][0]
        elif name == "place":
            nears = [made["norm two", c][0] for c in each]
            fars = [swap(x, "mp", 1) for x in nears]
            made[name] = ready = place(chunks, where, nears, fars, n, after)

    for k in each:
        run("forward", k)
        if k:
            run("sum two", k - 1)
    if not last:
        run("sum two", 0)
    run("norm two", 0)
    if last:
        run("sum two", last)
        run("norm two", 1)
    run("back", 0)
    for k in each[1:]:
        if k > 1:
            run("norm two", k)
            run("sum one", k - 1)
        run("back", k)
        if k == 1:
            run("sum one", 0)
    run("weights", 0)
    if not last:
        run("sum one", 0)
    run("norm one", 0)
    if last:
        run("sum one", last)
    for k in each:
        if k:
            run("norm one", k)
        if k == 1:
            run("place", 0)
        run("mix", k)
        if k < last:
            run("attend", k)
        if k == max(last - 1, 0):
            run("weight sums", 0)
    run("values", 0)
    run("attend", last)

    layer_out = made["place"]
    dv, value_parts = made["values"]
    dqs, dk = [made["attend", k][0] for k in each], made["attend", last][1]
    picks = [made["mix", k][1] for k in each]
    sums = add_sums(
        [made["norm one", k][2] for k in each], [made["norm two", k][2] for k in each],
        [made["back", k][3] for k in each],
    )
    far_sums = swap(sums, "mp", 1)
    state = {"values": value_parts, "weights": made["weights"]}
    steps = {"values": 0, "keys": 0, "weights": min(1, len(bits) - 1)}

    def advance(name):
        nonlocal ready
        k = steps[name]
        if k < len(bits):
            state[name] = sum_step(k, *state[name], ready)
            if k + 1 == len(bits) and name != "weights":
                state[name] = [state[name][0].astype(bf16)]
        elif k < 2 * len(bits) - 1:
            held = state[name][0]
            state[name] = [join(held, swap(held, "dp", bits[2 * len(bits) - 1 - k]), (ready,))]
        ready = state[name][0]
        steps[name] += 1

    shares = me ^ jnp.array([0, 2, 1, 3], jnp.int32)
    key_parts = key_project(chunks, order, dqs, dk, dv, tokens, sums, far_sums, (ready,))
    state["keys"], ready = key_parts, key_parts[0]
    if stepwise:
        advance("values")
        advance("weights")
    here, there = input_grads(chunks, shares, dqs, dk, dv, wq, wk, wv, (ready,))
    send, keep = token_grads(chunks, here, swap(there, "mp", 1), picks, (here,))
    ready = send
    if stepwise:
        for name in TURNS:
            advance(name)
        while steps["weights"] < len(bits):
            advance("weights")
        for name in ("values", "keys"):
            while steps[name] < 2 * len(bits) - 1:
                advance(name)
        grads = state["weights"][0]
        grad_w_in, grad_w_down = grads[0, 0], grads[0, 1]
        value_parts, key_parts = (
            (state[name][0], swap(state[name][0], "dp", bits[0])) for name in ("values", "keys")
        )
    else:
        grad_w_in, grad_w_down = (
            lax.psum_scatter(
                made["weights"][0][0, k].astype(f32), "dp", scatter_dimension=0, tiled=True
            )
            for k in range(2)
        )
        value_parts, key_parts = (
            [lax.psum(part.astype(f32), "dp").astype(bf16) for part in parts_of]
            for parts_of in (value_parts, key_parts)
        )
    grad_tokens = add_wide(keep, swap(send, "mp", 2), (ready,))
    gv, go = settle(order, value_parts, w, after=(grad_tokens,))
    gq, gk, g1, s1, bo, g2, s2, bd, bi, bq, bk, bv = settle(order, key_parts, w, sums=True, after=(gv,))
    return (
        layer_out, grad_tokens.T, gq.T, bq, gk.T, bk, gv.T, bv,
        go, bo, g1, s1, grad_w_in, bi, grad_w_down.T, bd, g2, s2,
    )


def solution(mesh):
    in_specs = (
        P("dp", None), P("dp", None),
        P(None, "mp"), P("mp"), P(None, "mp"), P("mp"), P(None, "mp"), P("mp"),
        P("mp", None), P(), P(), P(),
        P("dp", "mp"), P("mp"), P("mp", "dp"), P(), P(), P(),
        P("dp", None),
    )
    out_specs = (
        P("dp", None), P("dp", "mp"),
        P(None, "mp"), P("mp"), P(None, "mp"), P("mp"), P(None, "mp"), P("mp"),
        P("mp", None), P(), P(), P(),
        P("dp", "mp"), P("mp"), P("mp", "dp"), P(), P(), P(),
    )
    return jax.shard_map(shards, mesh=mesh, in_specs=in_specs, out_specs=out_specs, check_vma=False)
```

```python
from functools import partial
import math

import jax
import jax.numpy as jnp
from jax import lax
from jax.experimental import pallas as pl
from jax.experimental.pallas import tpu as pltpu
from jax.sharding import PartitionSpec as P

HEAD_DIM = 64
HALF_DIM = HEAD_DIM // 2
WIDE = 128
USED = 80
MASKED = -1e30
LOG2E = math.log2(math.e)
EPS = 1e-12
BLOCK = 256
B_OUT, GAIN1, SHIFT1, B_IN, B_DOWN, GAIN2, SHIFT2 = (slice(k, k + 1) for k in range(7))
bf16 = jnp.bfloat16
f32 = jnp.float32
VMEM = pl.BlockSpec(memory_space=pltpu.VMEM)
SMEM = pl.BlockSpec(memory_space=pltpu.SMEM)
ANY = pl.BlockSpec(memory_space=pl.ANY)
HBM = pl.BlockSpec(memory_space=pltpu.HBM)
TURNS = (
    "values", "keys", "values", "weights", "keys", "values", "keys", "values", "keys", "keys"
)
SHARE = 1e9


def launch(body, args, in_specs, out_shape, out_specs, *, mib, us, after=(), scalars=0, grid=(), scratch=(), aliases=None):
    taken, waits = len(args), len(after)

    def run(*refs):
        body(*refs[:taken], *refs[taken + waits :])

    return pl.pallas_call(
        run,
        grid_spec=pltpu.PrefetchScalarGridSpec(
            num_scalar_prefetch=scalars,
            grid=grid,
            in_specs=list(in_specs) + [ANY] * waits,
            out_specs=out_specs,
            scratch_shapes=list(scratch),
        ),
        out_shape=out_shape,
        input_output_aliases=aliases or {},
        compiler_params=pltpu.CompilerParams(vmem_limit_bytes=mib * 2**20),
        cost_estimate=pl.CostEstimate(flops=int(us * SHARE), bytes_accessed=0, transcendentals=0),
    )(*args, *after)


def out(*shape, dtype=bf16):
    return jax.ShapeDtypeStruct(shape, dtype)


def dot(left, right, left_dim, right_dim):
    return lax.dot_general(
        left, right, (((left_dim,), (right_dim,)), ((), ())), preferred_element_type=f32
    )


def qkv_body(
    len_ref, tok_hbm, wq_hbm, wk_hbm, wv_hbm, bq_ref, bk_ref, bv_ref,
    qa_ref, ka_ref, va_ref, cos_ref, sin_ref, tok_ref, w_ref, sems,
):
    copies = [
        pltpu.make_async_copy(from_ref, to_ref, sems.at[k])
        for k, (from_ref, to_ref) in enumerate((
            (tok_hbm, tok_ref), (wq_hbm, w_ref.at[0]), (wk_hbm, w_ref.at[1]), (wv_hbm, w_ref.at[2])
        ))
    ]
    for copy in copies:
        copy.start()
    n = tok_ref.shape[0]
    heads = w_ref.shape[1] // HEAD_DIM
    pos = lax.broadcasted_iota(jnp.int32, (1, n), 1)
    first = len_ref[0, 0]
    used = first + len_ref[0, 1]
    in0, in1 = pos < first, pos < used
    start = jnp.where(in0, 0, jnp.where(in1, first, used))
    index = lax.broadcasted_iota(jnp.int32, (HALF_DIM, 1), 0).astype(f32)
    freq = jnp.exp(index * (-math.log(10000.0) / HALF_DIM))
    angles = freq * (pos - start).astype(f32)
    cosine, sine = jnp.cos(angles), jnp.sin(angles)
    cos_ref[...] = cosine
    sin_ref[...] = sine
    segment = jnp.where(in0, 0, jnp.where(in1, 1, 2))
    row = lax.broadcasted_iota(jnp.int32, (WIDE - HEAD_DIM, n), 0)
    same = row == segment
    q_tail = jnp.where(same, 1.0, 0.0).astype(bf16)
    k_tail = jnp.where(jnp.logical_or(same, row > 2), 0.0, MASKED).astype(bf16)
    v_tail = jnp.where(row < 3, 1.0, 0.0).astype(bf16)

    def rotated(lin, h, scale):
        a = lin[h * HEAD_DIM : h * HEAD_DIM + HALF_DIM]
        b = lin[h * HEAD_DIM + HALF_DIM : (h + 1) * HEAD_DIM]
        x, y = a * cosine - b * sine, b * cosine + a * sine
        if scale != 1.0:
            x, y = x * scale, y * scale
        return x.astype(bf16), y.astype(bf16)

    copies[0].wait()
    for k, (b_ref, to_ref, tail, scale) in enumerate((
        (bq_ref, qa_ref, q_tail, LOG2E / math.sqrt(HEAD_DIM)),
        (bk_ref, ka_ref, k_tail, 1.0),
        (bv_ref, va_ref, v_tail, None),
    )):
        copies[1 + k].wait()
        column = jnp.broadcast_to(b_ref[...].reshape(1, -1), (8, b_ref.shape[0])).T[:, 0:1]
        lin = dot(w_ref[k], tok_ref[...], 1, 1) + column
        for h in range(heads):
            if scale is None:
                to_ref[h, 0:HEAD_DIM] = lin[h * HEAD_DIM : (h + 1) * HEAD_DIM].astype(bf16)
            else:
                x, y = rotated(lin, h, scale)
                to_ref[h, 0:HALF_DIM] = x
                to_ref[h, HALF_DIM:HEAD_DIM] = y
            to_ref[h, HEAD_DIM:] = tail


def project(lengths, tok, wq, wk, wv, bq, bk, bv):
    n = tok.shape[0]
    heads = wq.shape[0] // HEAD_DIM
    return launch(
        qkv_body, (lengths, tok, wq, wk, wv, bq, bk, bv), [SMEM] + [HBM] * 4 + [VMEM] * 3,
        (
            out(heads, WIDE, n), out(heads, WIDE, n), out(heads, WIDE, n),
            out(HALF_DIM, n, dtype=f32), out(HALF_DIM, n, dtype=f32),
        ),
        (VMEM,) * 5, mib=63, us=5,
        scratch=[
            pltpu.VMEM(tok.shape, bf16), pltpu.VMEM((3, *wq.shape), bf16),
            pltpu.SemaphoreType.DMA((4,)),
        ],
    )


def chunk_block(chunk, half_blocks):
    first, count = chunk
    return lambda i: (i // count) * half_blocks + first + lax.rem(i, count)


def attend_body(qa_ref, ka_ref, va_ref, p_ref, mix_ref, inv_ref):
    heads, _, n = ka_ref.shape
    pieces = [slice(at, at + n // 3) for at in range(0, n, n // 3)]

    def score(h):
        scores = [dot(ka_ref[h, :, piece], qa_ref[h], 0, 0) for piece in pieces]
        top = jnp.max(scores[0], axis=0, keepdims=True)
        for s in scores[1:]:
            top = jnp.maximum(top, jnp.max(s, axis=0, keepdims=True))
        return scores, top

    def mix(h, scores, top):
        mixed = None
        for piece, s in zip(pieces, scores):
            p = jnp.exp2(s - top).astype(bf16)
            p_ref[h, piece] = p
            term = jnp.dot(va_ref[h, 0:USED, piece], p, preferred_element_type=f32)
            mixed = term if mixed is None else mixed + term
        inv = 1.0 / mixed[HEAD_DIM : HEAD_DIM + 1]
        mix_ref[h * HEAD_DIM : (h + 1) * HEAD_DIM] = (mixed[0:HEAD_DIM] * inv).astype(bf16)
        inv_ref[h] = inv

    following = score(0)
    for h in range(heads):
        current = following
        if h + 1 < heads:
            following = score(h + 1)
        mix(h, *current)


def attend(chunk, qa, ka, va, after=()):
    heads, _, n = qa.shape
    block = chunk_block(chunk, n // BLOCK // 2)
    steps = 2 * chunk[1]
    width = steps * BLOCK
    return launch(
        attend_body, (qa, ka, va),
        [pl.BlockSpec((heads, WIDE, BLOCK), lambda i: (0, 0, block(i))), VMEM, VMEM],
        (out(heads, n, width), out(heads * HEAD_DIM, width), out(heads, 1, width, dtype=f32)),
        (
            pl.BlockSpec((heads, n, BLOCK), lambda i: (0, 0, i)),
            pl.BlockSpec((heads * HEAD_DIM, BLOCK), lambda i: (0, i)),
            pl.BlockSpec((heads, 1, BLOCK), lambda i: (0, 0, i)),
        ),
        mib=56, us=2.4 * steps, grid=(steps,), after=after,
    )


def attend_back_body(
    last, do_ref, mix_ref, inv_ref, qa_ref, ka_ref, va_ref, p_ref, cos_ref, sin_ref, *refs
):
    if last:
        cos_all, sin_all, before, dq_ref, to_ref, dk_ref = refs
        held = ((dk_ref, before),)
    else:
        *before, dq_ref, dk_ref, dv_ref = refs
        held = tuple(zip((dk_ref, dv_ref), before or (None, None)))
    heads, _, width = qa_ref.shape
    n = ka_ref.shape[2]
    pieces = [slice(at, at + n // 3) for at in range(0, n, n // 3)]

    @pl.when(pl.program_id(0) == 0)
    def _():
        for acc, start in held:
            acc[...] = jnp.zeros_like(acc) if start is None else start[...]

    def score_grad(h):
        rows = slice(h * HEAD_DIM, (h + 1) * HEAD_DIM)
        do = (do_ref[rows].astype(f32) * inv_ref[h]).astype(bf16)
        delta = jnp.sum(do.astype(f32) * mix_ref[rows].astype(f32), axis=0, keepdims=True)
        d1 = delta.astype(bf16).astype(f32)
        d2 = (delta - d1).astype(bf16).astype(f32)
        d3 = delta - d1 - d2
        row = lax.broadcasted_iota(jnp.int32, (USED - HEAD_DIM, width), 0)
        tail = jnp.where(row == 0, -d1, jnp.where(row == 1, -d2, jnp.where(row == 2, -d3, 0.0)))
        do_wide = jnp.concatenate([do, tail.astype(bf16)], axis=0)
        return do, [dot(va_ref[h, 0:USED, piece], do_wide, 0, 0) for piece in pieces]

    def finish(h, do, grads):
        lo, mid, hi = h * HEAD_DIM, h * HEAD_DIM + HALF_DIM, (h + 1) * HEAD_DIM
        dq = None
        for piece, dp in zip(pieces, grads):
            p = p_ref[h, piece]
            ds = (p.astype(f32) * dp).astype(bf16)
            term = jnp.dot(ka_ref[h, 0:HEAD_DIM, piece], ds, preferred_element_type=f32)
            dq = term if dq is None else dq + term
            dk_ref[lo:hi, piece] += dot(qa_ref[h, 0:HEAD_DIM], ds, 1, 1)
            if not last:
                dv_ref[lo:hi, piece] += dot(do, p, 1, 1)
        dq = dq * (1.0 / math.sqrt(HEAD_DIM))
        dq_ref[lo:mid], dq_ref[mid:hi] = turned_back(
            dq[0:HALF_DIM], dq[HALF_DIM:HEAD_DIM], cos_ref[...], sin_ref[...]
        )

    following = score_grad(0)
    for h in range(heads):
        current = following
        if h + 1 < heads:
            following = score_grad(h + 1)
        finish(h, *current)
    if last:

        @pl.when(pl.program_id(0) == pl.num_programs(0) - 1)
        def _():
            for lo in range(0, dk_ref.shape[0], HEAD_DIM):
                mid, hi = lo + HALF_DIM, lo + HEAD_DIM
                a, b = dk_ref[lo:mid] * math.log(2.0), dk_ref[mid:hi] * math.log(2.0)
                to_ref[lo:mid], to_ref[mid:hi] = turned_back(a, b, cos_all[...], sin_all[...])


def turned_back(a, b, cosine, sine):
    return (a * cosine + b * sine).astype(bf16), (b * cosine - a * sine).astype(bf16)


def attend_back(chunk, do, mix, inv, qa, ka, va, p, cosine, sine, before, last, after=()):
    heads, _, n = qa.shape
    w = heads * HEAD_DIM
    block = chunk_block(chunk, n // BLOCK // 2)
    steps = 2 * chunk[1]
    columns = pl.BlockSpec((w, BLOCK), lambda i: (0, i))
    table = pl.BlockSpec((HALF_DIM, BLOCK), lambda i: (0, block(i)))
    before = (cosine, sine, *before) if last else before
    shapes = (out(w, steps * BLOCK), out(w, n)) if last else (
        out(w, steps * BLOCK), out(w, n, dtype=f32), out(w, n, dtype=f32)
    )
    return launch(
        partial(attend_back_body, last),
        (do, mix, inv, qa, ka, va, p, cosine, sine, *before),
        [
            columns,
            columns,
            pl.BlockSpec((heads, 1, BLOCK), lambda i: (0, 0, i)),
            pl.BlockSpec((heads, WIDE, BLOCK), lambda i: (0, 0, block(i))),
            VMEM,
            VMEM,
            pl.BlockSpec((heads, n, BLOCK), lambda i: (0, 0, i)),
            table,
            table,
        ] + [VMEM] * len(before),
        shapes, (columns,) + (VMEM,) * (len(shapes) - 1),
        mib=46, us=3 * steps, grid=(steps,), after=after,
        scratch=[pltpu.VMEM((w, n), f32)] if last else (),
    )


def value_grad_body(do_ref, inv_ref, p_ref, before, to_ref, acc):
    step = pl.program_id(0)

    @pl.when(step == 0)
    def _():
        acc[...] = before[...]

    for h in range(p_ref.shape[0]):
        rows = slice(h * HEAD_DIM, (h + 1) * HEAD_DIM)
        do = (do_ref[rows].astype(f32) * inv_ref[h]).astype(bf16)
        acc[rows] += dot(do, p_ref[h], 1, 1)

    @pl.when(step == pl.num_programs(0) - 1)
    def _():
        to_ref[...] = acc[...].astype(bf16)


def value_grad(do, inv, p, before, after=()):
    heads, n, width = p.shape
    w = heads * HEAD_DIM
    return launch(
        value_grad_body, (do, inv, p, before),
        [
            pl.BlockSpec((w, BLOCK), lambda i: (0, i)),
            pl.BlockSpec((heads, 1, BLOCK), lambda i: (0, 0, i)),
            pl.BlockSpec((heads, n, BLOCK), lambda i: (0, 0, i)),
            VMEM,
        ],
        out(w, n), VMEM, mib=20, us=2, grid=(width // BLOCK,), after=after,
        scratch=[pltpu.VMEM((w, n), f32)],
    )


def by_run(chunk, other):
    return lambda i, where: lax.rem(where[0] + other, 2) * chunk[1] + i


def assemble(order, pieces, which, after=()):
    rows, d = pieces[0].shape[2:]
    count, parts = len(pieces), sum(piece.shape[0] for piece in pieces)

    def body(order_ref, *refs):
        to_ref = refs[count]
        held = [(ref, k) for ref in refs[0:count] for k in range(ref.shape[0])]
        for j, (ref, k) in enumerate(held):
            to_ref[pl.ds(pl.multiple_of(order_ref[j] * rows, rows), rows)] = ref[k, which]

    return launch(
        body, (order, *pieces), [SMEM] + [VMEM] * count, out(parts * rows, d), VMEM,
        mib=12, us=0.6, after=after,
    )


def hold(arrays, after=()):
    count = len(arrays)

    def body(*refs):
        for from_ref, to_ref in zip(refs[:count], refs[count:]):
            to_ref[...] = from_ref[...]

    return launch(
        body, arrays, [VMEM] * count, tuple(out(*x.shape) for x in arrays), (VMEM,) * count,
        mib=8, us=0.5, after=after,
    )


def add_body(a_ref, b_ref, to_ref):
    to_ref[...] = (a_ref[...].astype(f32) + b_ref[...].astype(f32)).astype(bf16)


def add_low(a, b, after=()):
    return launch(
        add_body, (a, b), [VMEM] * 2, out(*a.shape), VMEM, mib=8, us=0.5, after=after
    )


def add_parts(keep, came, last, after=()):
    parts, *shape = keep.shape

    def body(keep_ref, came_ref, *to_refs):
        result = keep_ref[...].astype(f32) + came_ref[...].astype(f32)
        if last:
            to_refs[0][...] = result
        else:
            to_refs[0][...] = result[0 : parts // 2].astype(bf16)
            to_refs[1][...] = result[parts // 2 :].astype(bf16)

    shapes = (out(*keep.shape, dtype=f32),) if last else (out(parts // 2, *shape),) * 2
    return launch(
        body, (keep, came), [VMEM] * 2, shapes, (VMEM,) * len(shapes), mib=12, us=0.8, after=after
    )


def add_wide(a, b, after=()):
    def body(a_ref, b_ref, to_ref):
        to_ref[...] = a_ref[...] + b_ref[...].astype(f32)

    return launch(
        body, (a, b), [VMEM] * 2, out(*a.shape, dtype=f32), VMEM, mib=8, us=0.8, after=after
    )


def stack_rows(vectors, after=()):
    def body(*refs):
        *from_refs, to_ref = refs
        to_ref[...] = jnp.zeros_like(to_ref)
        for k, ref in enumerate(from_refs):
            to_ref[k : k + 1] = ref[...].reshape(1, -1)

    return launch(
        body, tuple(vectors), [VMEM] * len(vectors), out(8, vectors[0].shape[0], dtype=f32), VMEM,
        mib=4, us=1, after=after,
    )


def join_body(a_ref, b_ref, to_ref):
    k = a_ref.shape[0]
    to_ref[0:k] = a_ref[...]
    to_ref[k:] = b_ref[...]


def join(a, b, after=()):
    return launch(
        join_body, (a, b), [VMEM, VMEM], out(a.shape[0] + b.shape[0], *a.shape[1:]), VMEM,
        mib=8, us=0.5, after=after,
    )


def forward_body(*refs):
    where_ref, *refs = refs
    mixes, outs = refs[0:8], refs[8:12]
    (tok_ref, vec_ref, wi_ref, wd_ref,
     low_ref, unit_ref, scale_ref, act_ref, slope_ref, own_ref, other_ref) = refs[12:]

    def norm(k):
        z = tok_ref[k].astype(f32) + vec_ref[B_OUT]
        for mix_ref, wo_ref in zip(mixes[k::2], outs):
            z = z + dot(mix_ref[...], wo_ref[...], 0, 0)
        center = z - jnp.mean(z, axis=-1, keepdims=True)
        scale = lax.rsqrt(jnp.mean(center * center, axis=-1, keepdims=True) + EPS)
        unit = center * scale
        low = (unit * vec_ref[GAIN1] + vec_ref[SHIFT1]).astype(bf16)
        low_ref[k] = low
        if k == 0:
            unit_ref[...] = unit.astype(bf16)
            scale_ref[...] = scale
        return low

    def expand(k, low):
        return jnp.dot(low, wi_ref[...], preferred_element_type=f32) + vec_ref[B_IN]

    def activate(k, inner):
        phi = 0.5 * lax.erf(inner * math.sqrt(0.5)) + 0.5
        bell = jnp.exp2(inner * inner * (-0.5 * LOG2E)) * (1.0 / math.sqrt(2.0 * math.pi))
        act = (inner * phi).astype(bf16)
        act_ref[k] = act
        slope_ref[k] = (phi + inner * bell).astype(bf16)
        return act

    def contract(k, act):
        (own_ref, other_ref)[k][...] = dot(act, wd_ref[...], 1, 1).astype(bf16)

    low_b = norm(1)
    inner_b = expand(1, low_b)
    low_a = norm(0)
    act_b = activate(1, inner_b)
    inner_a = expand(0, low_a)
    contract(1, act_b)
    contract(0, activate(0, inner_a))


def split_tokens(chunks, where, tok, after=()):
    n, d = tok.shape
    runs = slot_runs(chunks, n)

    def body(where_ref, tok_ref, *to_refs):
        for to_ref, (first, _, length) in zip(to_refs, runs):
            for k in range(2):
                half = where_ref[0] if k == 0 else 1 - where_ref[0]
                at = pl.multiple_of(half * (n // 2) + first, BLOCK)
                to_ref[k] = tok_ref[pl.ds(at, length)]

    return launch(
        body, (where, tok), [SMEM, VMEM], tuple(out(2, length, d) for _, _, length in runs),
        (VMEM,) * len(runs), mib=12, us=1, after=after,
    )


def feed_forward(chunk, where, mixes, outs, tok, vec, wi, wd, after=()):
    _, _, d = tok.shape
    hidden = wi.shape[1]
    count = chunk[1]
    rows = count * BLOCK
    w = mixes[0].shape[0]
    own_run, other_run = by_run(chunk, 0), by_run(chunk, 1)
    mix_specs, mix_args = [], []
    for m in mixes:
        mix_specs += [
            pl.BlockSpec((w, BLOCK), lambda i, where: (0, own_run(i, where))),
            pl.BlockSpec((w, BLOCK), lambda i, where: (0, other_run(i, where))),
        ]
        mix_args += [m, m]
    both = lambda width: pl.BlockSpec((2, BLOCK, width), lambda i, where: (0, i, 0))
    one = lambda width: pl.BlockSpec((BLOCK, width), lambda i, where: (i, 0))
    return launch(
        forward_body, (where, *mix_args, *outs, tok, vec, wi, wd),
        mix_specs + [VMEM] * 4 + [
            pl.BlockSpec((2, BLOCK, d), lambda i, where: (0, i, 0)),
        ] + [VMEM] * 3,
        (
            out(2, rows, d), out(rows, d), out(rows, 1, dtype=f32), out(2, rows, hidden),
            out(2, rows, hidden), out(rows, d), out(rows, d),
        ),
        (both(d), one(d), one(1), both(hidden), both(hidden), one(d), one(d)),
        mib=24, us=4.5 * count, scalars=1, grid=(count,), after=after,
    )


def norm_back(g, unit, scale, gain):
    q = g * gain
    return scale * (
        q - jnp.mean(q, axis=-1, keepdims=True) - unit * jnp.mean(q * unit, axis=-1, keepdims=True)
    )


def put_sums(sums_ref, *terms):
    sums_ref[...] = jnp.zeros_like(sums_ref)
    for k, term in enumerate(terms):
        sums_ref[k : k + 1] = jnp.sum(term, axis=0, keepdims=True)


def second_norm_body(
    first, where_ref, len_ref, unit_ref, mine_ref, theirs_ref, vec_ref, cot_ref,
    out_ref, low_ref, sums_ref, held, sem,
):
    rows = unit_ref.shape[0]
    half = cot_ref.shape[0] // 2
    start = pl.multiple_of(where_ref[0] * half + first, BLOCK)
    copy = pltpu.make_async_copy(cot_ref.at[pl.ds(start, rows)], held, sem)
    copy.start()
    total = mine_ref[...].astype(f32) + theirs_ref[...].astype(f32)
    z = unit_ref[...].astype(f32) * vec_ref[GAIN1] + vec_ref[SHIFT1] + total + vec_ref[B_DOWN]
    center = z - jnp.mean(z, axis=-1, keepdims=True)
    scale = lax.rsqrt(jnp.mean(center * center, axis=-1, keepdims=True) + EPS)
    unit = center * scale
    out_ref[...] = (unit * vec_ref[GAIN2] + vec_ref[SHIFT2]).astype(bf16)
    slot = start + lax.broadcasted_iota(jnp.int32, (rows, 1), 0)
    copy.wait()
    g = jnp.where(slot < len_ref[0, 0] + len_ref[0, 1], held[...], 0.0)
    back = norm_back(g, unit, scale, vec_ref[GAIN2])
    low_ref[...] = back.astype(bf16)
    put_sums(sums_ref, g * unit, g, back)


def second_norm(chunk, where, lengths, unit, mine, theirs, vec, cot, after=()):
    rows, d = unit.shape
    return launch(
        partial(second_norm_body, chunk[0] * BLOCK),
        (where, lengths, unit, mine, theirs, vec, cot), [SMEM] * 2 + [VMEM] * 4 + [HBM],
        (out(rows, d), out(rows, d), out(8, d, dtype=f32)), (VMEM,) * 3,
        mib=12, us=2, after=after,
        scratch=[pltpu.VMEM((rows, d), f32), pltpu.SemaphoreType.DMA(())],
    )


def first_norm_body(unit_ref, scale_ref, vec_ref, skip_ref, mine_ref, theirs_ref, low_ref, sums_ref):
    g = skip_ref[...].astype(f32) + (mine_ref[...].astype(f32) + theirs_ref[...].astype(f32))
    unit = unit_ref[...].astype(f32)
    back = norm_back(g, unit, scale_ref[...], vec_ref[GAIN1])
    low_ref[...] = back.astype(bf16)
    put_sums(sums_ref, g * unit, g, back)


def first_norm(unit, scale, vec, skip, mine, theirs, after=()):
    rows, d = skip.shape
    return launch(
        first_norm_body, (unit, scale, vec, skip, mine, theirs), [VMEM] * 6,
        (out(rows, d), out(8, d, dtype=f32)), (VMEM,) * 2, mib=12, us=1, after=after,
    )


def backward_body(near_ref, far_ref, wi_ref, wd_ref, slope_ref, gi_ref, own_ref, other_ref, sums_ref):
    def open_up(k):
        return jnp.dot((near_ref, far_ref)[k][...], wd_ref[...], preferred_element_type=f32)

    def slopes(k, g):
        g = (g * slope_ref[k].astype(f32)).astype(bf16)
        gi_ref[k] = g
        return g

    def close(k, g):
        (own_ref, other_ref)[k][...] = dot(g, wi_ref[...], 1, 1).astype(bf16)

    open_b = open_up(1)
    open_a = open_up(0)
    g_b = slopes(1, open_b)
    close(1, g_b)
    g_a = slopes(0, open_a)
    close(0, g_a)
    put_sums(sums_ref, g_a.astype(f32) + g_b.astype(f32))


def feed_back(near_low, far_low, wi, wd, slope, after=()):
    rows, d = near_low.shape
    hidden = slope.shape[2]
    return launch(
        backward_body, (near_low, far_low, wi, wd, slope), [VMEM] * 5,
        (out(2, rows, hidden), out(rows, d), out(rows, d), out(8, hidden, dtype=f32)),
        (VMEM,) * 4, mib=12, us=1.6, after=after,
    )


def weight_grad_body(order_ref, *refs):
    chunks = (len(refs) - 2) // 5 if len(refs) % 5 == 2 else (len(refs) - 3) // 5
    lows, gis, acts = refs[0:chunks], refs[chunks : 2 * chunks], refs[2 * chunks : 3 * chunks]
    nears, fars = refs[3 * chunks : 4 * chunks], refs[4 * chunks : 5 * chunks]
    *to_refs, grad_ref = refs[5 * chunks :]

    def spread(which):
        first = to_refs[0].shape[0]
        rows = to_refs[0].shape[2]
        for j in range(order_ref.shape[0]):
            to_ref, k = (to_refs[0], j) if j < first else (to_refs[1], j - first)
            at = pl.ds(pl.multiple_of(order_ref[j] * rows, rows), rows)
            to_ref[k, which] = grad_ref[at].astype(bf16)

    total = None
    for low_ref, gi_ref in zip(lows, gis):
        for k in range(2):
            term = dot(low_ref[k], gi_ref[k], 0, 0)
            total = term if total is None else total + term
    grad_ref[...] = total
    spread(0)
    total = None
    for near_ref, far_ref, act_ref in zip(nears, fars, acts):
        term = dot(near_ref[...], act_ref[0], 0, 0) + dot(far_ref[...], act_ref[1], 0, 0)
        total = term if total is None else total + term
    grad_ref[...] = total
    spread(1)


def weight_grads(order, lows, gis, acts, nears, fars, after=()):
    d, hidden = lows[0].shape[2], gis[0].shape[2]
    width = BLOCK
    parts = order.shape[0]
    sizes = (1,) if parts == 1 else (parts // 2, parts // 2)
    rows = d // parts
    wide = [pl.BlockSpec((2, a.shape[1], width), lambda i, order: (0, 0, i)) for a in gis]
    return launch(
        weight_grad_body, (order, *lows, *gis, *acts, *nears, *fars),
        [VMEM] * len(lows) + wide + wide + [VMEM] * (2 * len(lows)),
        tuple(out(k, 2, rows, hidden) for k in sizes),
        tuple(pl.BlockSpec((k, 2, rows, width), lambda i, order: (0, 0, 0, i)) for k in sizes),
        mib=20, us=6, scalars=1, grid=(hidden // width,),
        scratch=[pltpu.VMEM((d, width), f32)], after=after,
    )


def mix_back_body(where_ref, near_ref, far_ref, wo_ref, mix_ref, do_ref, pick_ref, gwo_ref):
    w, d = wo_ref.shape

    @pl.when(pl.program_id(0) == 0)
    def _():
        gwo_ref[...] = jnp.zeros_like(gwo_ref)

    row = lax.broadcasted_iota(jnp.int32, (w, d), 0) + where_ref[1] * w
    chosen = jnp.where(row == lax.broadcasted_iota(jnp.int32, (w, d), 1), 1.0, 0.0).astype(bf16)

    def run(from_ref):
        g = from_ref[...]
        do_ref[...] = dot(wo_ref[...], g, 1, 1).astype(bf16)
        pick_ref[...] = dot(chosen, g, 1, 1).astype(bf16)
        gwo_ref[...] += jnp.dot(mix_ref[...], g, preferred_element_type=f32)

    @pl.when(pl.program_id(0) == where_ref[0])
    def _():
        run(near_ref)

    @pl.when(pl.program_id(0) != where_ref[0])
    def _():
        run(far_ref)


def mix_back(where, near_half, far_half, wo, mix, after=()):
    rows, d = near_half.shape
    w = wo.shape[0]
    columns = pl.BlockSpec((w, rows), lambda i, where: (0, i))
    return launch(
        mix_back_body, (where, near_half, far_half, wo, mix), [VMEM, VMEM, VMEM, columns],
        (out(w, 2 * rows), out(w, 2 * rows), out(w, d, dtype=f32)),
        (columns, columns, pl.BlockSpec((w, d), lambda i, where: (0, 0))),
        mib=12, us=2, scalars=1, grid=(2,), after=after,
    )


def slot_runs(chunks, n):
    return [(first * BLOCK, n // 2 + first * BLOCK, count * BLOCK) for first, count in chunks]


def spread(order_ref, grad_ref, to_refs, rows):
    first = to_refs[0].shape[0]
    for j in range(order_ref.shape[0]):
        to_ref, k = (to_refs[0], j) if j < first else (to_refs[1], j - first)
        at = pl.ds(pl.multiple_of(order_ref[j] * rows, rows), rows)
        to_ref[k, 0:rows] = grad_ref[at].astype(bf16)


def total(refs):
    result = refs[0][...]
    for ref in refs[1:]:
        result = result + ref[...]
    return result


def split_parts(order):
    parts = order.shape[0]
    return (1,) if parts == 1 else (parts // 2, parts // 2)


def value_project(order, dv, tok, gwos, after=()):
    w, d = gwos[0].shape
    sizes = split_parts(order)
    count = len(gwos)

    def body(order_ref, dv_ref, tok_ref, *refs):
        *to_refs, grad_ref = refs[count:]
        grad_ref[0:w] = jnp.dot(dv_ref[...], tok_ref[...], preferred_element_type=f32)
        grad_ref[w:] = total(refs[0:count])
        spread(order_ref, grad_ref, to_refs, 2 * w // order_ref.shape[0])

    return launch(
        body, (order, dv, tok, *gwos), [SMEM] + [VMEM] * (2 + count),
        tuple(out(k, 2 * w // sum(sizes), d) for k in sizes), (VMEM,) * len(sizes),
        mib=16, us=1.5, scratch=[pltpu.VMEM((2 * w, d), f32)], after=after,
    )


def key_project(chunks, order, dqs, dk, dv, tok, sums, far_sums, after=()):
    w, n = dk.shape
    d = tok.shape[1]
    sizes = split_parts(order)
    count = len(dqs)
    parts = sum(sizes)
    rows = 2 * w // parts
    runs = slot_runs(chunks, n)

    def body(order_ref, dk_ref, dv_ref, tok_ref, sums_ref, far_ref, *refs):
        dq_refs, (*to_refs, grad_ref, vec_ref) = refs[0:count], refs[count:]
        ones = jnp.ones((8, n), bf16)
        grad = row = None
        for dq_ref, (first, second, length) in zip(dq_refs, runs):
            bias = dot(ones[:, 0 : 2 * length], dq_ref[...], 1, 1)
            row = bias if row is None else row + bias
            for k, at in enumerate((first, second)):
                term = jnp.dot(
                    dq_ref[:, k * length : (k + 1) * length], tok_ref[at : at + length],
                    preferred_element_type=f32,
                )
                grad = term if grad is None else grad + term
        grad_ref[0:w] = grad
        grad_ref[w:] = jnp.dot(dk_ref[...], tok_ref[...], preferred_element_type=f32)
        vec_ref[...] = sums_ref[...]
        vec_ref[0:6] = sums_ref[0:6] + far_ref[0:6]
        biases = [row, dot(ones, dk_ref[...], 1, 1), dot(ones, dv_ref[...], 1, 1)]
        biases.append(jnp.zeros((8, d - 3 * w), f32))
        vec_ref[7:8] = jnp.concatenate(biases, axis=1)[0:1]
        spread(order_ref, grad_ref, to_refs, rows)
        for j in range(parts):
            to_ref, k = (to_refs[0], j) if j < sizes[0] else (to_refs[1], j - sizes[0])
            tail = vec_ref[...] if parts == 1 else jnp.broadcast_to(
                vec_ref[pl.ds(order_ref[j], 1)], (8, d)
            )
            to_ref[k, rows:] = jnp.concatenate([tail, tail], axis=0).astype(bf16)

    return launch(
        body, (order, dk, dv, tok, sums, far_sums, *dqs), [SMEM] + [VMEM] * (5 + count),
        tuple(out(k, rows + 16, d) for k in sizes), (VMEM,) * len(sizes),
        mib=16, us=2, after=after,
        scratch=[pltpu.VMEM((2 * w, d), f32), pltpu.VMEM((8, d), f32)],
    )


def add_sums(ones, twos, ins, after=()):
    count = len(ones)

    def body(*refs):
        to_ref = refs[-1]
        to_ref[...] = jnp.zeros_like(to_ref)
        to_ref[0:3] = total([ref for ref in refs[0:count]])[0:3]
        to_ref[3:6] = total([ref for ref in refs[count : 2 * count]])[0:3]
        to_ref[6:7] = total([ref for ref in refs[2 * count : 3 * count]])[0:1]

    return launch(
        body, (*ones, *twos, *ins), [VMEM] * (3 * count), out(*ones[0].shape, dtype=f32), VMEM,
        mib=4, us=0.5, after=after,
    )


def input_grad_body(runs, share_ref, dk_ref, dv_ref, wq_ref, wk_ref, wv_ref, *refs):
    *dqs, here_ref, there_ref, all_ref = refs
    w = dk_ref.shape[0]
    for dq_ref, (first, second, length) in zip(dqs, runs):
        for k, at in enumerate((first, second)):
            slots = slice(at, at + length)
            part = dot(wq_ref[...], dq_ref[:, k * length : (k + 1) * length], 0, 0)
            part = part + dot(wk_ref[...], dk_ref[:, slots], 0, 0)
            all_ref[:, slots] = part + dot(wv_ref[...], dv_ref[:, slots], 0, 0)
    for j in range(4):
        at = pl.ds(pl.multiple_of(share_ref[j] * w, w), w)
        to_ref = here_ref if j < 2 else there_ref
        to_ref[j % 2] = all_ref[at].astype(bf16)


def input_grads(chunks, shares, dqs, dk, dv, wq, wk, wv, after=()):
    w, d = wq.shape
    n = dk.shape[1]
    return launch(
        partial(input_grad_body, slot_runs(chunks, n)), (shares, dk, dv, wq, wk, wv, *dqs),
        [SMEM] + [VMEM] * (5 + len(chunks)), (out(2, w, n), out(2, w, n)), (VMEM, VMEM),
        mib=20, us=3, scratch=[pltpu.VMEM((d, n), f32)], after=after,
    )


def token_grad_body(runs, here_ref, there_ref, *refs):
    *picks, send_ref, keep_ref = refs
    send_ref[...] = (here_ref[1].astype(f32) + there_ref[1].astype(f32)).astype(bf16)
    for pick_ref, (first, second, length) in zip(picks, runs):
        for k, at in enumerate((first, second)):
            slots = slice(at, at + length)
            keep_ref[:, slots] = (
                here_ref[0, :, slots].astype(f32) + there_ref[0, :, slots].astype(f32)
                + pick_ref[:, k * length : (k + 1) * length].astype(f32)
            )


def token_grads(chunks, here, there, picks, after=()):
    _, w, n = here.shape
    return launch(
        partial(token_grad_body, slot_runs(chunks, n)), (here, there, *picks),
        [VMEM] * (2 + len(chunks)), (out(w, n), out(w, n, dtype=f32)), (VMEM, VMEM),
        mib=12, us=1.5, after=after,
    )


def settle(order, pieces, w, sums=False, after=()):
    d = pieces[0].shape[-1]
    count, parts = len(pieces), order.shape[0]
    rows = 2 * w // parts

    def body(order_ref, *refs):
        from_refs, to_refs, all_ref, vec_ref = refs[0:count], refs[count:-2], refs[-2], refs[-1]
        held = [(ref, k) for ref in from_refs for k in range(ref.shape[0])]
        for j, (ref, k) in enumerate(held):
            at = pl.ds(pl.multiple_of(order_ref[j] * rows, rows), rows)
            all_ref[at] = ref[k, 0:rows].astype(f32)
            if sums:
                tail = ref[k, rows:].astype(f32)
                if parts == 1:
                    vec_ref[...] = tail[0:8]
                else:
                    vec_ref[pl.ds(order_ref[j], 1)] = tail[0:1]
        to_refs[0][...] = all_ref[0:w]
        to_refs[1][...] = all_ref[w:]
        if sums:
            for k in range(7):
                to_refs[2 + k][...] = vec_ref[k : k + 1].reshape(d)
            for k in range(3):
                to_refs[9 + k][...] = vec_ref[7:8, k * w : (k + 1) * w].reshape(w)

    shapes = (out(w, d, dtype=f32),) * 2
    if sums:
        shapes += (out(d, dtype=f32),) * 7 + (out(w, dtype=f32),) * 3
    return launch(
        body, (order, *pieces), [SMEM] + [VMEM] * count, shapes, (VMEM,) * len(shapes),
        mib=12, us=1, after=after,
        scratch=[pltpu.VMEM((2 * w, d), f32), pltpu.VMEM((8, d), f32)],
    )


def place_body(runs, where_ref, *refs):
    count = len(runs)
    nears, fars, to_ref = refs[0:count], refs[count : 2 * count], refs[-1]
    core = where_ref[0]
    half = to_ref.shape[0] // 2
    for near_ref, far_ref, (first, _, length) in zip(nears, fars, runs):
        for ref, owner in ((near_ref, core), (far_ref, 1 - core)):
            at = pl.ds(pl.multiple_of(owner * half + first, BLOCK), length)
            to_ref[at] = ref[...]


def place(chunks, where, nears, fars, n, after=()):
    d = nears[0].shape[1]
    return launch(
        partial(place_body, slot_runs(chunks, n)), (where, *nears, *fars),
        [SMEM] + [VMEM] * (2 * len(chunks)), out(n, d), VMEM, mib=12, us=2, after=after,
    )


def swap(x, axis, bit):
    return lax.ppermute(x, axis, [(i, i ^ bit) for i in range(lax.axis_size(axis))])


def split_slots(n):
    half_blocks = n // BLOCK // 2
    first = 0
    return [(0, first), (first, half_blocks - first)] if first else [(k, 1) for k in range(half_blocks)]


def shards(
    tokens, lengths, w_query, b_query, w_key, b_key, w_value, b_value, w_out, b_out, ln1_gain,
    ln1_bias, w_in, b_in, w_down, b_down, ln2_gain, ln2_bias, cotangent,
):
    dp = lax.axis_size("dp")
    n, d = tokens.shape
    w = w_query.shape[1]
    chunks = split_slots(n)
    me = lax.axis_index("mp")
    core = me % 2
    where = jnp.stack([core, me]).astype(jnp.int32)
    wq, wk, wv = w_query.T, w_key.T, w_value.T

    stepwise = dp & (dp - 1) == 0 and dp > 1 and (d // dp) % 16 == 0
    bits = [1 << k for k in range(dp.bit_length() - 1)] if stepwise else []
    parts = 1 << len(bits)
    order = jnp.zeros((1,), jnp.int32)
    if stepwise:
        count = len(bits)
        places = [
            sum(bit for k, bit in enumerate(bits) if j >> (count - 1 - k) & 1) for j in range(parts)
        ]
        order = lax.axis_index("dp") ^ jnp.array(places, jnp.int32)

    def sum_step(k, keep, send, *after):
        return add_parts(keep, swap(send, "dp", bits[k]), k + 1 == len(bits), after)

    vec = stack_rows([b_out, ln1_gain, ln1_bias, b_in, b_down, ln2_gain, ln2_bias])
    qa, ka, va, cosine, sine = project(lengths, tokens, wq, wk, wv, b_query, b_key, b_value)
    out_y = swap(w_out, "mp", 2)
    outs = (w_out, out_y, swap(w_out, "mp", 1), swap(out_y, "mp", 1))

    each, last = range(len(chunks)), len(chunks) - 1
    kept, mixes = [], []

    def run_attend(k, *after):
        kept.append(attend(chunks[k], qa, ka, va, after))
        mix = kept[k][1]
        mix_y = swap(mix, "mp", 2)
        mixes.append((mix, mix_y, swap(mix, "mp", 1), swap(mix_y, "mp", 1)))
        return kept[k][2]

    both = jnp.stack([w_in, w_down.T])[None]
    if stepwise:
        near, far, held = [both], [swap(both, "dp", bits[0])], both
        step = list(reversed(bits[1:]))

        def fetch(k, *after):
            nonlocal held, ready
            came = swap(held, "dp", step[k])
            if k + 1 < len(step):
                held = ready = join(held, came, (*after, far[-1]))
            else:
                (came,) = hold((came,), (*after, far[-1]))
                ready = came
            near.append(came)
            far.append(swap(came, "dp", bits[0]))

        ready = cosine
        for k in each:
            ready = run_attend(k, ready)
            if k < len(step):
                fetch(k, ready)
        for k in range(len(near) - 1, len(step)):
            fetch(k, ready)
        gathered = near + far
    else:
        ready = cosine
        for k in each:
            ready = run_attend(k, ready)
        gathered = [jnp.stack([
            lax.all_gather(part, "dp", axis=0, tiled=True) for part in (w_in, w_down.T)
        ])[None]]
    token_runs = split_tokens(chunks, where, tokens, (ready,))
    out_near, out_y = hold((w_out, out_y), (ready,))
    outs = (out_near, out_y, *outs[2:])
    came = [mix[1] for mix in mixes] + [token_runs[0], out_near]
    wi, wd = (assemble(order, gathered, k, (ready, *came)) for k in range(2))

    made = {}

    def run(name, k, *waits):
        nonlocal ready
        after = (ready, *waits)
        if name == "forward":
            made[name, k] = feed_forward(
                chunks[k], where, mixes[k], outs, token_runs[k], vec, wi, wd, after
            )
            ready = made[name, k][2]
        elif name == "sum two":
            *_, own, other = made["forward", k]
            mine = ready = add_low(own, swap(other, "mp", 1), after)
            made[name, k] = mine, swap(mine, "mp", 2)
        elif name == "norm two":
            made[name, k] = second_norm(
                chunks[k], where, lengths, made["forward", k][1], *made["sum two", k], vec,
                cotangent, after,
            )
            made["low", k] = made[name, k][1], swap(made[name, k][1], "mp", 1)
            ready = made[name, k][2]
        elif name == "back":
            made[name, k] = feed_back(*made["low", k], wi, wd, made["forward", k][4], after)
            ready = made[name, k][3]
        elif name == "sum one":
            _, own, other, _ = made["back", k]
            mine = ready = add_low(own, swap(other, "mp", 1), after)
            made[name, k] = mine, swap(mine, "mp", 2)
        elif name == "weights":
            forwards = [made["forward", c] for c in range(len(chunks))]
            nears, fars = zip(*(made["low", c] for c in range(len(chunks))))
            made[name] = weight_grads(
                order, [f[0] for f in forwards], [made["back", c][0] for c in range(len(chunks))],
                [f[3] for f in forwards], nears, fars, after,
            )
            ready = made[name][0]
        elif name == "norm one":
            forward = made["forward", k]
            half, sums = first_norm(
                forward[1], forward[2], vec, made["low", k][0], *made["sum one", k], after
            )
            made[name, k] = half, swap(half, "mp", 1), sums
            ready = sums
        elif name == "mix":
            made[name, k] = mix_back(where, *made["norm one", k][0:2], out_near, kept[k][1], after)
            ready = made[name, k][0]
        elif name == "values":
            gwos = [made["mix", c][2] for c in each]
            dv = value_grad(
                made["mix", last][0], kept[last][2], kept[last][0], made["attend", last - 1][2], after
            )
            made[name] = dv, value_project(order, dv, tokens, gwos)
            ready = made[name][1][0]
        elif name == "attend":
            p, mix, inv = kept[k]
            before = made[name, k - 1][1 : 2 if k == last else 3] if k else ()
            made[name, k] = attend_back(
                chunks[k], made["mix", k][0], mix, inv, qa, ka, va, p, cosine, sine, before,
                k == last, after,
            )
            ready = made[name, k][0]
        elif name == "weight sums":
            if stepwise and k < len(bits) - 1:
                made["weights"] = sum_step(k, *made["weights"], *after)
                ready = made["weights"][0]
        elif name == "place":
            nears = [made["norm two", c][0] for c in each]
            fars = [swap(x, "mp", 1) for x in nears]
            made[name] = ready = place(chunks, where, nears, fars, n, after)

    for k in each:
        run("forward", k)
        if k:
            run("sum two", k - 1)
    if not last:
        run("sum two", 0)
    run("norm two", 0)
    if last:
        run("sum two", last)
        run("norm two", 1)
    run("back", 0)
    for k in each[1:]:
        if k > 1:
            run("norm two", k)
            run("sum one", k - 1)
        run("back", k)
        if k == 1:
            run("sum one", 0)
    run("weights", 0)
    if not last:
        run("sum one", 0)
    run("norm one", 0)
    if last:
        run("sum one", last)
    for k in each:
        if k:
            run("norm one", k)
        if k == 1:
            run("place", 0)
        run("mix", k)
        if k < last:
            run("attend", k)
        if k == max(last - 1, 0):
            run("weight sums", 0)
    run("values", 0)
    run("attend", last)

    layer_out = made["place"]
    dv, value_parts = made["values"]
    dqs, dk = [made["attend", k][0] for k in each], made["attend", last][1]
    picks = [made["mix", k][1] for k in each]
    sums = add_sums(
        [made["norm one", k][2] for k in each], [made["norm two", k][2] for k in each],
        [made["back", k][3] for k in each],
    )
    far_sums = swap(sums, "mp", 1)
    state = {"values": value_parts, "weights": made["weights"]}
    steps = {"values": 0, "keys": 0, "weights": min(1, len(bits) - 1)}

    def advance(name):
        nonlocal ready
        k = steps[name]
        if k < len(bits):
            state[name] = sum_step(k, *state[name], ready)
            if k + 1 == len(bits) and name != "weights":
                state[name] = [state[name][0].astype(bf16)]
        elif k < 2 * len(bits) - 1:
            held = state[name][0]
            state[name] = [join(held, swap(held, "dp", bits[2 * len(bits) - 1 - k]), (ready,))]
        ready = state[name][0]
        steps[name] += 1

    shares = me ^ jnp.array([0, 2, 1, 3], jnp.int32)
    key_parts = key_project(chunks, order, dqs, dk, dv, tokens, sums, far_sums, (ready,))
    state["keys"], ready = key_parts, key_parts[0]
    if stepwise:
        advance("values")
        advance("weights")
    here, there = input_grads(chunks, shares, dqs, dk, dv, wq, wk, wv, (ready,))
    send, keep = token_grads(chunks, here, swap(there, "mp", 1), picks, (here,))
    ready = send
    if stepwise:
        for name in TURNS:
            advance(name)
        while steps["weights"] < len(bits):
            advance("weights")
        for name in ("values", "keys"):
            while steps[name] < 2 * len(bits) - 1:
                advance(name)
        grads = state["weights"][0]
        grad_w_in, grad_w_down = grads[0, 0], grads[0, 1]
        value_parts, key_parts = (
            (state[name][0], swap(state[name][0], "dp", bits[0])) for name in ("values", "keys")
        )
    else:
        grad_w_in, grad_w_down = (
            lax.psum_scatter(
                made["weights"][0][0, k].astype(f32), "dp", scatter_dimension=0, tiled=True
            )
            for k in range(2)
        )
        value_parts, key_parts = (
            [lax.psum(part.astype(f32), "dp").astype(bf16) for part in parts_of]
            for parts_of in (value_parts, key_parts)
        )
    grad_tokens = add_wide(keep, swap(send, "mp", 2), (ready,))
    gv, go = settle(order, value_parts, w, after=(grad_tokens,))
    gq, gk, g1, s1, bo, g2, s2, bd, bi, bq, bk, bv = settle(order, key_parts, w, sums=True, after=(gv,))
    return (
        layer_out, grad_tokens.T, gq.T, bq, gk.T, bk, gv.T, bv,
        go, bo, g1, s1, grad_w_in, bi, grad_w_down.T, bd, g2, s2,
    )


def solution(mesh):
    in_specs = (
        P("dp", None), P("dp", None),
        P(None, "mp"), P("mp"), P(None, "mp"), P("mp"), P(None, "mp"), P("mp"),
        P("mp", None), P(), P(), P(),
        P("dp", "mp"), P("mp"), P("mp", "dp"), P(), P(), P(),
        P("dp", None),
    )
    out_specs = (
        P("dp", None), P("dp", "mp"),
        P(None, "mp"), P("mp"), P(None, "mp"), P("mp"), P(None, "mp"), P("mp"),
        P("mp", None), P(), P(), P(),
        P("dp", "mp"), P("mp"), P("mp", "dp"), P(), P(), P(),
    )
    return jax.shard_map(shards, mesh=mesh, in_specs=in_specs, out_specs=out_specs, check_vma=False)
```
